512 devices in a mesh: tile: 64 (over x, z, core), trc: 8 (over y).
Axes of the slice: x: 4, y: 8, z: 8, core: 2. Of those that a mesh axis runs over, the one named last changes fastest.
Arguments:
- cotangent: float32 [56, 16, 128, 1024], P('trc', None, 'tile'), may hold values from -0.5 to 2.5
- uptake_rate: bfloat16 [56, 8, 128, 1024], P('trc', None, 'tile'), may hold values from 0.049804688 to 2
- nutrient: float32 [8, 128, 1024], P(None, 'tile'), may hold values from 0.02 to 5
- depth_levels: int32 [128, 1024], P('tile'), may hold values from 0 to 16, as said below
- region_ids: int32 [128, 1024], P('tile'), may hold values from 0 to 63
- uptake_matrix: bfloat16 [56, 56], replicated, may hold values from -0.75 to 0.75
- province_rates: float32 [64, 56], P(None, 'trc'), may hold values from 0.2 to 2
- half_saturation: float32 [56], P('trc'), may hold values from 0.1 to 1
- biharmonic: float32 [56], P('trc'), may hold values from 0.003 to 0.025
- sinking: float32 [56], P('trc'), may hold values from 0.05 to 0.6
Outputs:
- tracer_grad: float32 [56, 16, 128, 1024], P('trc', None, 'tile')
- rate_grad: float32 [64, 56], P('tile', 'trc')
The draws below stay inside these ranges and needn't reach their ends.
Inputs may be any that keep to these rules, and one draw needn't show every extreme that they name: `depth_levels`: on some device every column is wet and one of its columns has all 16 levels wet; every device has at least 256 wet columns, and some devices have dry ones.
All inputs are finite; a program needn't handle non-finite values.
Results may differ from the reference program's by a relative error of at most 0.0014.
Values may be sent and summed in bfloat16 or wider, within the bound.
No kernel may reach another device: no remote copies, remote signals or barrier semaphores. Data moves between devices by JAX's collectives and lax.ppermute only.
A program may use at most 64 MiB of HBM per device.

```python
import math
import jax
import jax.numpy as jnp
from jax import lax

NTR = 56
REG = 64
LEV = 16
EUPH = 8
RX = 2
NYG = 1024
NX = 128


def draw_depth_levels(key, part):
    tile_count = NX // RX
    columns = RX * NYG
    key_shift, key_full, key_order, key_depth = jax.random.split(key, 4)
    shifts = jax.random.randint(key_shift, (tile_count,), 0, 4)
    full_tile = jax.random.randint(key_full, (), 0, tile_count)
    tile_ids = jnp.arange(tile_count)
    shifts = jnp.where(tile_ids == full_tile, 0, shifts)
    shifts = jnp.where(tile_ids == (full_tile + 1) % tile_count, 3, shifts)
    counts = jnp.right_shift(jnp.full((tile_count,), columns, jnp.int32), shifts.astype(jnp.int32))
    orders = jax.vmap(lambda subkey: jax.random.permutation(subkey, columns))(jax.random.split(key_order, tile_count))
    depths = jax.random.randint(key_depth, (tile_count, columns), 1, LEV + 1)
    deepest = (tile_ids[:, None] == full_tile) & (orders == 0)
    depths = jnp.where(deepest, LEV, depths)
    levels = jnp.where(orders < counts[:, None], depths, 0)
    return levels.reshape(NX, NYG).astype(jnp.int32)


def draw_region_ids(key, part):
    span = REG // (NX // RX)
    key_near, key_far, key_pick = jax.random.split(key, 3)
    tile_of_row = jnp.arange(NX) // RX
    offsets = jax.random.randint(key_near, (NX, NYG), 0, span + 1)
    near_ids = (tile_of_row[:, None] * span + offsets) % REG
    far_ids = jax.random.randint(key_far, (NX, NYG), 0, REG)
    picks = jax.random.randint(key_pick, (NX, NYG), 0, 8) == 0
    return jnp.where(picks, far_ids, near_ids).astype(jnp.int32)


def level_of(key, extent, shards, least, largest):
    gain = 1.0
    for dim, shards_of in shards:
        heights = jax.random.uniform(jax.random.fold_in(jax.random.fold_in(key, 6), dim), (shards_of,), jnp.float32, least / len(shards), largest / len(shards))
        gain = gain * jnp.repeat(jnp.exp(heights), extent[dim] // shards_of).reshape((-1,) + (1,) * (len(extent) - 1 - dim))
    return gain


def centred(key, extent, width, most, held_as=jnp.bfloat16):
    return jnp.clip(width * jax.random.normal(key, extent, jnp.float32), -most, most).astype(held_as)


def setup_inputs(seed: int = 0) -> dict:
    key_of = jax.random.split(jax.random.key(seed), 11)
    return {
        "cotangent": jnp.clip(-0.5 + 3.0 * jax.random.uniform(key_of[0], (NTR, LEV, NX, NYG), jnp.float32) ** level_of(key_of[0], (NTR, LEV, NX, NYG), ((0, 8), (2, 64)), -0.2, 0.2), -0.5, 2.5),
        "uptake_rate": jnp.clip(jnp.exp(math.log(2.0) - 3.6927934 * jax.random.uniform(key_of[1], (NTR, EUPH, NX, NYG), jnp.float32) ** level_of(key_of[1], (NTR, EUPH, NX, NYG), ((0, 8), (2, 64)), -0.2, 0.2)), 0.049804688, 2.0).astype(jnp.bfloat16),
        "nutrient": jnp.clip(jnp.exp(math.log(5.0) - 5.521461 * jax.random.uniform(key_of[2], (EUPH, NX, NYG), jnp.float32) ** level_of(key_of[2], (EUPH, NX, NYG), ((1, 64),), -0.2, 0.2)), 0.02, 5.0),
        "depth_levels": draw_depth_levels(jax.random.fold_in(key_of[10], 71), 0),
        "region_ids": draw_region_ids(jax.random.fold_in(key_of[10], 71), 0),
        "uptake_matrix": centred(key_of[5], (NTR, NTR), NTR ** -0.5, 0.75),
        "province_rates": jnp.clip(jnp.exp(math.log(2.0) - 2.3025851 * jax.random.uniform(key_of[6], (REG, NTR), jnp.float32) ** level_of(key_of[6], (REG, NTR), ((1, 8),), -0.2, 0.2)), 0.2, 2.0),
        "half_saturation": jnp.clip(jnp.exp(math.log(1.0) - 2.3025851 * jax.random.uniform(key_of[7], (NTR,), jnp.float32) ** level_of(key_of[7], (NTR,), ((0, 8),), -0.2, 0.2)), 0.1, 1.0),
        "biharmonic": jnp.clip(jnp.exp(math.log(0.025) - 2.1202635 * jax.random.uniform(key_of[8], (NTR,), jnp.float32) ** level_of(key_of[8], (NTR,), ((0, 8),), -0.2, 0.2)), 0.003, 0.025),
        "sinking": jnp.clip(0.05 + 0.55 * jax.random.uniform(key_of[9], (NTR,), jnp.float32) ** level_of(key_of[9], (NTR,), ((0, 8),), -0.2, 0.2), 0.05, 0.6),
    }


def laplacian(values, wet_cells):
    padded = jnp.pad(values, ((0, 0), (1, 1), (0, 0)))
    padded_wet = jnp.pad(wet_cells, ((0, 0), (1, 1), (0, 0)))
    northern = padded[:, 2:]
    southern = padded[:, :-2]
    north_wet = padded_wet[:, 2:]
    south_wet = padded_wet[:, :-2]
    eastern = jnp.roll(values, -1, 2)
    western = jnp.roll(values, 1, 2)
    east_wet = jnp.roll(wet_cells, -1, 2)
    west_wet = jnp.roll(wet_cells, 1, 2)
    return wet_cells * (north_wet * (northern - values) + south_wet * (southern - values)
                        + east_wet * (eastern - values) + west_wet * (western - values))


def reference(cotangent, uptake_rate, nutrient, depth_levels, region_ids, uptake_matrix,
              province_rates, half_saturation, biharmonic, sinking):
    level_ids = jnp.arange(LEV, dtype=jnp.int32)[:, None, None]
    wet_mask = (level_ids < depth_levels[None]).astype(jnp.float32)
    grad_wet = cotangent * wet_mask[None]
    limiter = nutrient[None] / (nutrient[None] + half_saturation[:, None, None, None])
    rate_cells = jnp.transpose(province_rates[region_ids], (2, 0, 1))
    weighted = (rate_cells[:, None] * limiter * grad_wet[:, :EUPH]).astype(jnp.bfloat16)
    cross_feed = jnp.dot(uptake_matrix.T, weighted.reshape(NTR, -1),
                         preferred_element_type=jnp.float32).reshape(NTR, EUPH, NX, NYG)
    column_term = jnp.sum(limiter * uptake_rate.astype(jnp.float32) * grad_wet[:, :EUPH], axis=1)
    province_ids = jnp.arange(REG, dtype=jnp.int32)[:, None, None]
    one_hot = (region_ids[None] == province_ids).astype(jnp.float32).reshape(REG, NX * NYG)
    rate_grad = jnp.dot(one_hot, column_term.reshape(NTR, NX * NYG).T, precision=lax.Precision.HIGHEST,
                        preferred_element_type=jnp.float32) * (1.0 / (EUPH * RX * NYG))

    def one_tracer(inputs):
        grad_one, cross_one, sink_one, mixing = inputs
        grad_mid = jnp.concatenate([grad_one[:EUPH] + wet_mask[:EUPH] * cross_one, grad_one[EUPH:]], axis=0)
        coupling = sink_one * wet_mask[:-1] * wet_mask[1:]
        grad_col = grad_mid + jnp.concatenate(
            [coupling * (grad_mid[1:] - grad_mid[:-1]), jnp.zeros((1, NX, NYG), jnp.float32)], axis=0)
        lap_once = laplacian(grad_col, wet_mask)
        return grad_col - mixing * laplacian(lap_once, wet_mask)

    tracer_grad = lax.map(one_tracer, (grad_wet, cross_feed, sinking, biharmonic))
    return tracer_grad, rate_grad
```

```python
import jax
import jax.numpy as jnp
from jax import lax
from jax.sharding import PartitionSpec as P

SCALE = 256.0


def shifted_sum(values, wet):
    eastern = jnp.roll(values, -1, 3)
    western = jnp.roll(values, 1, 3)
    east_wet = jnp.roll(wet, -1, 2)
    west_wet = jnp.roll(wet, 1, 2)
    return east_wet * (eastern - values) + west_wet * (western - values)


def laplacian(extended, extended_wet):
    centre = extended[:, :, 1:-1]
    centre_wet = extended_wet[:, 1:-1]
    return centre_wet * (
        extended_wet[:, 2:] * (extended[:, :, 2:] - centre)
        + extended_wet[:, :-2] * (extended[:, :, :-2] - centre)
        + shifted_sum(centre, centre_wet)
    )


def body(
    cotangent,
    uptake_rate,
    nutrient,
    depth_levels,
    region_ids,
    uptake_matrix,
    province_rates,
    half_saturation,
    biharmonic,
    sinking,
):
    own_count, levels, band_rows, zonal = cotangent.shape
    sunlit = uptake_rate.shape[1]
    columns = band_rows * zonal
    provinces = province_rates.shape[0]
    tiles = lax.axis_size("tile")
    up = [(i, i + 1) for i in range(tiles - 1)]
    down = [(i + 1, i) for i in range(tiles - 1)]
    depth_float = depth_levels.astype(jnp.float32)
    depth_south = lax.ppermute(depth_float, "tile", up)
    depth_north = lax.ppermute(depth_float, "tile", down)
    level_ids = lax.broadcasted_iota(jnp.int32, (levels, band_rows, zonal), 0)
    wet_mask = (level_ids < depth_levels[None]).astype(jnp.float32)
    grad_wet = cotangent * wet_mask[None]
    limiter = nutrient[None] / (nutrient[None] + half_saturation[:, None, None, None])
    province_ids = lax.broadcasted_iota(jnp.int32, (provinces, columns), 0)
    one_hot = (region_ids.reshape(1, columns) == province_ids).astype(jnp.float32)
    rate_cells = lax.dot_general(
        province_rates,
        one_hot,
        (((0,), (0,)), ((), ())),
        precision=lax.Precision.HIGHEST,
        preferred_element_type=jnp.float32,
    )
    weighted = (
        rate_cells.reshape(own_count, 1, band_rows, zonal) * limiter * grad_wet[:, :sunlit]
    ).astype(jnp.bfloat16)
    by_level = weighted.transpose(1, 0, 2, 3).reshape(sunlit, own_count, columns)
    all_tracers = lax.all_to_all(by_level, "trc", 0, 0, tiled=True)
    column_term = jnp.sum(limiter * uptake_rate.astype(jnp.float32) * grad_wet[:, :sunlit], axis=1)
    province_part = lax.dot_general(
        one_hot,
        column_term.reshape(own_count, columns),
        (((1,), (1,)), ((), ())),
        precision=lax.Precision.HIGHEST,
        preferred_element_type=jnp.float32,
    )
    own_parts = lax.all_to_all(province_part, "tile", 0, 0, tiled=True)
    rate_grad = jnp.sum(own_parts, axis=0, keepdims=True) * (1.0 / (sunlit * columns))
    fed = lax.dot_general(
        uptake_matrix,
        all_tracers.reshape(sunlit * own_count, columns),
        (((0,), (0,)), ((), ())),
        preferred_element_type=jnp.float32,
    )
    fed = (fed * SCALE).astype(jnp.float16).reshape(sunlit, own_count, columns)
    fed = lax.all_to_all(fed, "trc", 0, 0, tiled=True)
    cross_cells = (fed.astype(jnp.float32) * (1.0 / SCALE)).reshape(sunlit, own_count, band_rows, zonal)
    cross_cells = cross_cells.transpose(1, 0, 2, 3)
    grad_top = grad_wet[:, :sunlit] + wet_mask[None, :sunlit] * cross_cells
    grad_mid = jnp.concatenate([grad_top, grad_wet[:, sunlit:]], axis=1)
    coupling = sinking[:, None, None, None] * (wet_mask[:-1] * wet_mask[1:])[None]
    grad_col = grad_mid + jnp.concatenate(
        [
            coupling * (grad_mid[:, 1:] - grad_mid[:, :-1]),
            jnp.zeros((own_count, 1, band_rows, zonal), jnp.float32),
        ],
        axis=1,
    )
    halo = grad_col.astype(jnp.bfloat16)
    south = lax.ppermute(halo, "tile", up).astype(jnp.float32)
    north = lax.ppermute(halo, "tile", down).astype(jnp.float32)
    extended = jnp.concatenate([south, grad_col, north], axis=2)
    extended_depth = jnp.concatenate([depth_south, depth_float, depth_north], axis=0)
    row_levels = lax.broadcasted_iota(jnp.int32, (levels,) + extended_depth.shape, 0)
    extended_wet = (row_levels.astype(jnp.float32) < extended_depth[None]).astype(jnp.float32)
    lap_once = laplacian(extended, extended_wet)
    lap_twice = laplacian(lap_once, extended_wet[:, 1:-1])
    tracer_grad = grad_col - biharmonic[:, None, None, None] * lap_twice
    return (tracer_grad, rate_grad)


def solution(mesh):
    return jax.shard_map(
        body,
        mesh=mesh,
        in_specs=(
            P("trc", None, "tile", None),
            P("trc", None, "tile", None),
            P(None, "tile", None),
            P("tile", None),
            P("tile", None),
            P(),
            P(None, "trc"),
            P("trc"),
            P("trc"),
            P("trc"),
        ),
        out_specs=(P("trc", None, "tile", None), P("tile", "trc")),
        check_vma=False,
    )
```

```python
import jax
import jax.numpy as jnp
from jax import lax
from jax.experimental import pallas as pl
from jax.experimental.pallas import tpu as pltpu
from jax.sharding import PartitionSpec as P

SCALE = 256.0
LANES = 128
ROWS = 2
BF16 = jnp.bfloat16
F32 = jnp.float32
VMEM = pl.BlockSpec(memory_space=pltpu.VMEM)
SMEM = pl.BlockSpec(memory_space=pltpu.SMEM)
PARAMS = pltpu.CompilerParams(vmem_limit_bytes=40 * 1024 * 1024)


def row(ref, *at):
    *lead, r = at
    blocks = ref.shape[-2] // ROWS
    return ref[(*lead, pl.ds(r, blocks, stride=ROWS), slice(None))]


def wet_at(depth, level):
    return (depth > level).astype(F32)


def weighted_kernel(cot_ref, nutrient_ref, depth_ref, region_ref, rates_ref, half_ref, out_ref, table_ref):
    own, sunlit = out_ref.shape[1], out_ref.shape[0]
    blocks = cot_ref.shape[2] // ROWS
    provinces = rates_ref.shape[1]
    table_ref[...] = jnp.zeros(table_ref.shape, F32)
    table_ref[0:own, 0:provinces] = rates_ref[...]
    depth = [row(depth_ref, r) for r in range(ROWS)]
    region = [row(region_ref, r) for r in range(ROWS)]
    for t in range(own):
        line = jnp.broadcast_to(table_ref[t : t + 1, :], (blocks, LANES))
        rates = [jnp.take_along_axis(line, region[r], axis=1) for r in range(ROWS)]
        half = half_ref[t]
        for k in range(sunlit):
            rows = []
            for r in range(ROWS):
                food = row(nutrient_ref, k, r)
                limiter = food / (food + half)
                grad = row(cot_ref, t, k, r) * wet_at(depth[r], k)
                rows.append(rates[r] * limiter * grad)
            out_ref[k, t] = jnp.concatenate(rows, axis=0).astype(BF16)


def province_kernel(cot_ref, uptake_ref, nutrient_ref, depth_ref, region_ref, half_ref, out_ref, hot_ref, term_ref, parts_ref):
    provinces, own = out_ref.shape
    sunlit = nutrient_ref.shape[0]
    lines = depth_ref.shape[0]
    depth = depth_ref[...]
    for t in range(own):
        total = jnp.zeros((lines, LANES), F32)
        for k in range(sunlit):
            food = nutrient_ref[k]
            limiter = food / (food + half_ref[t])
            grad = cot_ref[t, k] * wet_at(depth, k)
            total = total + limiter * uptake_ref[t, k].astype(F32) * grad
        term_ref[pl.ds(t, lines, stride=8), :] = total
    ids = lax.broadcasted_iota(jnp.int32, (provinces, LANES), 0)
    for s in range(lines):
        line = jnp.broadcast_to(region_ref[s : s + 1, :], (provinces, LANES))
        hot_ref[:, s * LANES : (s + 1) * LANES] = (line == ids).astype(F32).astype(BF16)
        term = term_ref[s * 8 : (s + 1) * 8, :]
        high = term.astype(BF16).astype(F32)
        both = jnp.concatenate([high, term - high], axis=0)
        parts_ref[:, s * LANES : (s + 1) * LANES] = both.astype(BF16)
    sums = lax.dot_general(hot_ref[...], parts_ref[...], (((1,), (1,)), ((), ())), preferred_element_type=F32)
    out_ref[...] = sums[:, 0:own] + sums[:, 8 : 8 + own]


def feed_kernel(matrix_ref, weighted_ref, out_ref, wide_ref, fed_ref):
    tracers, lines = weighted_ref.shape[0], weighted_ref.shape[1]
    matrix = matrix_ref[...].astype(F32).T.astype(BF16)
    for t in range(tracers):
        wide_ref[t * lines : (t + 1) * lines, :] = weighted_ref[t].astype(F32)
    for s in range(0, lines, 2):
        cells = [wide_ref[pl.ds(s + i, tracers, stride=lines), :].astype(BF16) for i in range(2)]
        fed = jnp.dot(matrix, jnp.concatenate(cells, axis=1), preferred_element_type=F32) * SCALE
        for i in range(2):
            fed_ref[pl.ds(s + i, tracers, stride=lines), :] = fed[:, i * LANES : (i + 1) * LANES]
    for t in range(tracers):
        out_ref[t] = fed_ref[t * lines : (t + 1) * lines, :]


def column_kernel(cot_ref, fed_ref, depth_ref, sinking_ref, col_ref, halo_ref):
    own, levels = cot_ref.shape[0], cot_ref.shape[1]
    sunlit = fed_ref.shape[0]
    blocks = depth_ref.shape[0] // ROWS
    depth = [row(depth_ref, r) for r in range(ROWS)]
    halo_ref[own * levels] = jnp.concatenate(depth, axis=0).astype(F32).astype(BF16)

    def middle(t, k, r):
        wet = wet_at(depth[r], k)
        grad = row(cot_ref, t, k, r) * wet
        if k < sunlit:
            grad = grad + wet * (fed_ref[k, t, r * blocks : (r + 1) * blocks, :] * (1.0 / SCALE))
        return grad

    for t in range(own):
        sink = sinking_ref[t]
        below = [middle(t, levels - 1, r) for r in range(ROWS)]
        for k in range(levels - 1, -1, -1):
            rows = []
            if k == levels - 1:
                rows = below
            else:
                here = [middle(t, k, r) for r in range(ROWS)]
                for r in range(ROWS):
                    coupling = sink * wet_at(depth[r], k + 1)
                    rows.append(here[r] + coupling * (below[r] - here[r]))
                below = here
            both = jnp.concatenate(rows, axis=0)
            col_ref[t, k] = both
            halo_ref[t * levels + k] = both.astype(BF16)


def mixing_kernel(col_ref, south_ref, north_ref, depth_ref, mixing_ref, out_ref):
    own, levels = col_ref.shape[0], col_ref.shape[1]
    blocks = col_ref.shape[2] // ROWS
    lane_ids = lax.broadcasted_iota(jnp.int32, (blocks, LANES), 1)
    last_lane, first_lane = lane_ids == LANES - 1, lane_ids == 0

    def east(v):
        turned = pltpu.roll(v, LANES - 1, 1)
        return jnp.where(last_lane, pltpu.roll(turned, blocks - 1, 0), turned)

    def west(v):
        turned = pltpu.roll(v, 1, 1)
        return jnp.where(first_lane, pltpu.roll(turned, 1, 0), turned)

    def split(v):
        wide = v.astype(F32)
        return [wide[r * blocks : (r + 1) * blocks] for r in range(ROWS)]

    def laplacian(rows, edges_y, edges_x, lo, hi):
        flux = [edges_y[i] * (rows[i + 1] - rows[i]) for i in range(lo - 1, hi)]
        out = []
        for n, i in enumerate(range(lo, hi)):
            zonal = edges_x[i] * (east(rows[i]) - rows[i])
            out.append((flux[n + 1] - flux[n]) + (zonal - west(zonal)))
        return out

    own_depth = [row(depth_ref, r).astype(F32) for r in range(ROWS)]
    depths = split(south_ref[own * levels]) + own_depth + split(north_ref[own * levels])

    @pl.loop(0, levels)
    def _(k):
        at = lax.convert_element_type(k, F32)
        wet = [wet_at(d, at) for d in depths]
        edges_y = [wet[i] * wet[i + 1] for i in range(5)]
        edges_x = [None] + [wet[i] * east(wet[i]) for i in range(1, 5)]
        for t in range(own):
            here = split(col_ref[t, k])
            rows = split(south_ref[t * levels + k]) + here + split(north_ref[t * levels + k])
            once = laplacian(rows, edges_y, edges_x, 1, 5)
            twice = laplacian([None] + once, edges_y, edges_x, 2, 4)
            for r in range(ROWS):
                out_ref[t, k, pl.ds(r, blocks, stride=ROWS), :] = here[r] - mixing_ref[t] * twice[r]


def dense(band):
    *lead, rows, zonal = band.shape
    cut = band.reshape(*lead, rows, zonal // LANES, LANES)
    return jnp.swapaxes(cut, -3, -2).reshape(*lead, rows * zonal // LANES, LANES)


def undense(lines, rows):
    *lead, count, _ = lines.shape
    cut = lines.reshape(*lead, count // rows, rows, LANES)
    return jnp.swapaxes(cut, -3, -2).reshape(*lead, rows, count * LANES // rows)


def call(kernel, shapes, specs, scratch=()):
    return pl.pallas_call(
        kernel,
        out_shape=shapes,
        in_specs=specs,
        out_specs=jax.tree.map(lambda _: VMEM, shapes),
        scratch_shapes=scratch,
        compiler_params=PARAMS,
    )


def body(
    cotangent,
    uptake_rate,
    nutrient,
    depth_levels,
    region_ids,
    uptake_matrix,
    province_rates,
    half_saturation,
    biharmonic,
    sinking,
):
    own, levels, band_rows, zonal = cotangent.shape
    sunlit = uptake_rate.shape[1]
    columns = band_rows * zonal
    lines = columns // LANES
    provinces = province_rates.shape[0]
    tracers = uptake_matrix.shape[0]
    tiles = lax.axis_size("tile")
    up = [(i, i + 1) for i in range(tiles - 1)]
    down = [(i + 1, i) for i in range(tiles - 1)]
    shape = jax.ShapeDtypeStruct
    cot, uptake, nutrient = dense(cotangent), dense(uptake_rate), dense(nutrient)
    depth, region = dense(depth_levels), dense(region_ids)

    weighted = call(
        weighted_kernel,
        shape((sunlit, own, lines, LANES), BF16),
        [VMEM, VMEM, VMEM, VMEM, VMEM, SMEM],
        [pltpu.VMEM((8, LANES), F32)],
    )(cot, nutrient, depth, region, province_rates.T, half_saturation)
    all_tracers = lax.all_to_all(weighted, "trc", 0, 0, tiled=True).reshape(tracers, lines, LANES)
    province_part = call(
        province_kernel,
        shape((provinces, own), F32),
        [VMEM, VMEM, VMEM, VMEM, VMEM, SMEM],
        [
            pltpu.VMEM((provinces, columns), BF16),
            pltpu.VMEM((lines * 8, LANES), F32),
            pltpu.VMEM((16, columns), BF16),
        ],
    )(cot, uptake, nutrient, depth, region, half_saturation)
    own_parts = lax.all_to_all(province_part, "tile", 0, 0, tiled=True)
    rate_grad = jnp.sum(own_parts, axis=0, keepdims=True) * (1.0 / (sunlit * columns))
    fed = call(
        feed_kernel,
        shape((tracers, lines, LANES), F32),
        [VMEM, VMEM],
        [pltpu.VMEM((tracers * lines, LANES), F32), pltpu.VMEM((tracers * lines, LANES), F32)],
    )(uptake_matrix, all_tracers)
    fed = fed.astype(jnp.float16).reshape(sunlit, own, lines, LANES)
    fed = lax.all_to_all(fed, "trc", 0, 0, tiled=True).astype(F32)
    col, halo = call(
        column_kernel,
        (shape((own, levels, lines, LANES), F32), shape((own * levels + 1, lines, LANES), BF16)),
        [VMEM, VMEM, VMEM, SMEM],
    )(cot, fed, depth, sinking)
    south = lax.ppermute(halo, "tile", up)
    north = lax.ppermute(halo, "tile", down)
    tracer_grad = call(
        mixing_kernel,
        shape((own, levels, lines, LANES), F32),
        [VMEM, VMEM, VMEM, VMEM, SMEM],
    )(col, south, north, depth, biharmonic)
    return (undense(tracer_grad, band_rows), rate_grad)


def solution(mesh):
    return jax.shard_map(
        body,
        mesh=mesh,
        in_specs=(
            P("trc", None, "tile", None),
            P("trc", None, "tile", None),
            P(None, "tile", None),
            P("tile", None),
            P("tile", None),
            P(),
            P(None, "trc"),
            P("trc"),
            P("trc"),
            P("trc"),
        ),
        out_specs=(P("trc", None, "tile", None), P("tile", "trc")),
        check_vma=False,
    )
```

```python
import jax
import jax.numpy as jnp
from jax import lax
from jax.experimental import pallas as pl
from jax.experimental.pallas import tpu as pltpu
from jax.sharding import PartitionSpec as P

SCALE = 256.0
LANES = 128
ROWS = 2
SUB = 8
BF16 = jnp.bfloat16
F32 = jnp.float32
VMEM = pl.BlockSpec(memory_space=pltpu.VMEM)
HBM = pl.BlockSpec(memory_space=pltpu.HBM)
PARAMS = pltpu.CompilerParams(vmem_limit_bytes=40 * 1024 * 1024)


def row(ref, *at):
    *lead, r = at
    blocks = ref.shape[-2] // ROWS
    return ref[(*lead, pl.ds(r, blocks, stride=ROWS), slice(None))]


def wet_at(depth, level):
    return (depth > level).astype(F32)


def weighted_kernel(
    cot_hbm, nutrient_hbm, depth_hbm, region_hbm, rates_hbm, half_hbm, sinking_hbm, mixing_hbm,
    out_ref, params_ref,
    cot_ref, nutrient_ref, depth_ref, region_ref, rates_ref, half_ref, sinking_ref, mixing_ref, sems,
):
    own, sunlit = out_ref.shape[1], out_ref.shape[0]
    blocks = cot_ref.shape[2] // ROWS
    pairs = [
        (depth_hbm, depth_ref), (region_hbm, region_ref), (rates_hbm, rates_ref), (nutrient_hbm, nutrient_ref),
        (half_hbm, half_ref), (sinking_hbm, sinking_ref), (mixing_hbm, mixing_ref),
    ]
    pairs += [(cot_hbm.at[t, 0:sunlit], cot_ref.at[t]) for t in range(own)]
    copies = [pltpu.make_async_copy(here, there, sems.at[n]) for n, (here, there) in enumerate(pairs)]
    for copy in copies:
        copy.start()
    for copy in copies[: len(pairs) - own]:
        copy.wait()
    depth = [row(depth_ref, r) for r in range(ROWS)]
    region = [row(region_ref, r) for r in range(ROWS)]
    rest = jnp.zeros((1, LANES - rates_ref.shape[1]), F32)
    for t in range(own):
        line = jnp.concatenate([rates_ref[t : t + 1, :], rest], axis=1)
        line = jnp.broadcast_to(line, (blocks, LANES))
        rates = [jnp.take_along_axis(line, region[r], axis=1) for r in range(ROWS)]
        half = half_ref[t]
        for n, ref in enumerate((half_ref, sinking_ref, mixing_ref)):
            params_ref[n * SUB + t : n * SUB + t + 1, :] = jnp.full((1, LANES), ref[t], F32)
        copies[len(pairs) - own + t].wait()
        for k in range(sunlit):
            rows = []
            for r in range(ROWS):
                food = row(nutrient_ref, k, r)
                limiter = food / (food + half)
                grad = row(cot_ref, t, k, r) * wet_at(depth[r], k)
                rows.append(rates[r] * limiter * grad)
            out_ref[k, t] = jnp.concatenate(rows, axis=0).astype(BF16)


def province_kernel(cot_ref, uptake_ref, nutrient_ref, depth_ref, region_ref, params_ref, out_ref, hot_ref, term_ref, parts_ref):
    provinces, own = out_ref.shape
    sunlit = nutrient_ref.shape[0]
    lines = depth_ref.shape[0]
    depth = depth_ref[...]
    term_ref[...] = jnp.zeros(term_ref.shape, F32)
    for t in range(own):
        half = jnp.broadcast_to(params_ref[t : t + 1, :], (lines, LANES))
        total = jnp.zeros((lines, LANES), F32)
        for k in range(sunlit):
            food = nutrient_ref[k]
            limiter = food / (food + half)
            grad = cot_ref[t, k] * wet_at(depth, k)
            total = total + limiter * uptake_ref[t, k].astype(F32) * grad
        term_ref[pl.ds(t, lines, stride=8), :] = total
    ids = lax.broadcasted_iota(jnp.int32, (provinces, LANES), 0)
    for s in range(lines):
        line = jnp.broadcast_to(region_ref[s : s + 1, :], (provinces, LANES))
        hot_ref[:, s * LANES : (s + 1) * LANES] = (line == ids).astype(F32).astype(BF16)
        term = term_ref[s * 8 : (s + 1) * 8, :]
        high = term.astype(BF16).astype(F32)
        both = jnp.concatenate([high, term - high], axis=0)
        parts_ref[:, s * LANES : (s + 1) * LANES] = both.astype(BF16)
    sums = lax.dot_general(hot_ref[...], parts_ref[...], (((1,), (1,)), ((), ())), preferred_element_type=F32)
    out_ref[...] = sums[:, 0:own] + sums[:, 8 : 8 + own]


def feed_kernel(matrix_ref, weighted_ref, out_ref, wide_ref, fed_ref):
    tracers, lines = weighted_ref.shape[0], weighted_ref.shape[1]
    matrix = matrix_ref[...].astype(F32).T.astype(BF16)
    for t in range(tracers):
        wide_ref[t * lines : (t + 1) * lines, :] = weighted_ref[t].astype(F32)
    for s in range(0, lines, 2):
        cells = [wide_ref[pl.ds(s + i, tracers, stride=lines), :].astype(BF16) for i in range(2)]
        fed = jnp.dot(matrix, jnp.concatenate(cells, axis=1), preferred_element_type=F32) * SCALE
        for i in range(2):
            fed_ref[pl.ds(s + i, tracers, stride=lines), :] = fed[:, i * LANES : (i + 1) * LANES]
    for t in range(tracers):
        out_ref[t] = fed_ref[t * lines : (t + 1) * lines, :]


def column_kernel(cot_ref, fed_ref, depth_ref, params_ref, col_ref, halo_ref):
    lines = depth_ref.shape[0]
    blocks = lines // ROWS
    own = col_ref.shape[0] // lines
    levels = col_ref.shape[1]
    blocks_of = [depth_ref[b * ROWS + r : b * ROWS + r + 1, :] for r in range(ROWS) for b in range(blocks)]
    halo_ref[own * lines] = jnp.concatenate(blocks_of, axis=0).astype(F32).astype(BF16)
    ids = lax.broadcasted_iota(jnp.int32, (SUB, LANES), 0)
    bottom = ids == SUB - 1
    for n in range(lines):
        r, b = n // blocks, n % blocks
        depth = jnp.broadcast_to(blocks_of[n], (SUB, LANES))
        top_wet, low_wet = (depth > ids).astype(F32), (depth > ids + SUB).astype(F32)
        top_next = (depth > ids + 1).astype(F32)
        low_next = jnp.where(bottom, 0.0, (depth > ids + SUB + 1).astype(F32))

        for t in range(own):
            base = (t * levels) * lines + b * ROWS + r
            top = cot_ref[pl.ds(base, SUB, stride=lines), :] * top_wet
            low = cot_ref[pl.ds(base + SUB * lines, SUB, stride=lines), :] * low_wet
            fed = fed_ref[pl.ds(t * lines + n, SUB, stride=own * lines), :] * (1.0 / SCALE)
            top = top + top_wet * fed
            low_up = pltpu.roll(low, SUB - 1, 0)
            top_up = jnp.where(bottom, low_up, pltpu.roll(top, SUB - 1, 0))
            sink = params_ref[SUB + t : SUB + t + 1, :]
            col_top = top + sink * top_next * (top_up - top)
            col_low = low + sink * low_next * (low_up - low)
            both = jnp.concatenate([col_top, col_low], axis=0)
            col_ref[t * lines + n] = both
            halo_ref[t * lines + n] = both.astype(BF16)


def mixing_kernel(col_ref, south_ref, north_ref, depth_ref, params_ref, out_hbm, edges_y_ref, edges_x_ref, out_ref, sems):
    lines = depth_ref.shape[0]
    own = col_ref.shape[0] // lines
    blocks = lines // ROWS
    levels = col_ref.shape[1]
    halves = levels // SUB
    ids = lax.broadcasted_iota(jnp.int32, (SUB, LANES), 0)
    lane_ids = lax.broadcasted_iota(jnp.int32, (SUB, LANES), 1)
    last_lane, first_lane = lane_ids == LANES - 1, lane_ids == 0

    def east(v):
        turned = [pltpu.roll(x, LANES - 1, 1) for x in v]
        return [jnp.where(last_lane, turned[(b + 1) % blocks], turned[b]) for b in range(blocks)]

    def west(v):
        turned = [pltpu.roll(x, 1, 1) for x in v]
        return [jnp.where(first_lane, turned[(b - 1) % blocks], turned[b]) for b in range(blocks)]

    def own_depth(n):
        r, b = n // blocks, n % blocks
        return jnp.broadcast_to(depth_ref[b * ROWS + r : b * ROWS + r + 1, :], (SUB, LANES)).astype(F32)

    def field(which, at, h):
        ref = (south_ref, col_ref, north_ref)[at // ROWS]
        return [ref[which * lines + (at % ROWS) * blocks + b, h * SUB : (h + 1) * SUB, :].astype(F32) for b in range(blocks)]

    far = [ref[own * lines].astype(F32) for ref in (south_ref, north_ref)]
    for h in range(halves):
        at = (ids + h * SUB).astype(F32)
        wet = []
        for i in range(3 * ROWS):
            if i // ROWS == 1:
                depths = [own_depth((i % ROWS) * blocks + b) for b in range(blocks)]
            else:
                band, first = far[i // (2 * ROWS)], (i % ROWS) * blocks
                depths = [jnp.broadcast_to(band[first + b : first + b + 1], (SUB, LANES)) for b in range(blocks)]
            wet.append([(d > at).astype(F32) for d in depths])
        for i in range(3 * ROWS - 1):
            for b in range(blocks):
                edges_y_ref[h, i, b] = wet[i][b] * wet[i + 1][b]
        for i in range(1, 3 * ROWS - 1):
            ahead = east(wet[i])
            for b in range(blocks):
                edges_x_ref[h, i - 1, b] = wet[i][b] * ahead[b]

    def laplacian(rows, h, lo, hi):
        flux = [[edges_y_ref[h, i, b] * (rows[i + 1][b] - rows[i][b]) for b in range(blocks)] for i in range(lo - 1, hi)]
        out = []
        for n, i in enumerate(range(lo, hi)):
            ahead = east(rows[i])
            zonal = [edges_x_ref[h, i - 1, b] * (ahead[b] - rows[i][b]) for b in range(blocks)]
            behind = west(zonal)
            out.append([(flux[n + 1][b] - flux[n][b]) + (zonal[b] - behind[b]) for b in range(blocks)])
        return out

    def copy_out(t):
        part = pl.ds(t * levels * lines, levels * lines)
        return pltpu.make_async_copy(out_ref.at[part], out_hbm.at[part], sems.at[t])

    @pl.loop(0, own)
    def _(t):
        mixing = jnp.broadcast_to(params_ref[pl.ds(2 * SUB + t, 1), :], (SUB, LANES))
        for h in range(halves):
            rows = [field(t, i, h) for i in range(3 * ROWS)]
            once = laplacian(rows, h, 1, 5)
            twice = laplacian([None] + once, h, 2, 4)
            for r in range(ROWS):
                for b in range(blocks):
                    value = rows[ROWS + r][b] - mixing * twice[r][b]
                    out_ref[pl.ds((t * levels + h * SUB) * lines + b * ROWS + r, SUB, stride=lines), :] = value
        copy_out(t).start()

    for t in range(own):
        copy_out(t).wait()


def dense(band):
    *lead, rows, zonal = band.shape
    cut = band.reshape(*lead, rows, zonal // LANES, LANES)
    return jnp.swapaxes(cut, -3, -2).reshape(*lead, rows * zonal // LANES, LANES)


def undense(lines, rows):
    *lead, count, _ = lines.shape
    cut = lines.reshape(*lead, count // rows, rows, LANES)
    return jnp.swapaxes(cut, -3, -2).reshape(*lead, rows, count * LANES // rows)


def call(kernel, shapes, ins, outs, scratch=(), cost=None):
    return pl.pallas_call(
        kernel,
        out_shape=shapes,
        in_specs=ins,
        out_specs=outs,
        scratch_shapes=scratch,
        cost_estimate=cost,
        compiler_params=PARAMS,
    )


def body(
    cotangent,
    uptake_rate,
    nutrient,
    depth_levels,
    region_ids,
    uptake_matrix,
    province_rates,
    half_saturation,
    biharmonic,
    sinking,
):
    own, levels, band_rows, zonal = cotangent.shape
    sunlit = uptake_rate.shape[1]
    columns = band_rows * zonal
    lines = columns // LANES
    provinces = province_rates.shape[0]
    tracers = uptake_matrix.shape[0]
    tiles = lax.axis_size("tile")
    up = [(i, i + 1) for i in range(tiles - 1)]
    down = [(i + 1, i) for i in range(tiles - 1)]
    shape = jax.ShapeDtypeStruct
    cot, uptake, nutrient = dense(cotangent), dense(uptake_rate), dense(nutrient)
    depth, region = dense(depth_levels), dense(region_ids)

    inputs = (cot, nutrient, depth, region, province_rates.T, half_saturation, sinking, biharmonic)
    weighted, params = call(
        weighted_kernel,
        (shape((sunlit, own, lines, LANES), BF16), shape((3 * SUB, LANES), F32)),
        [HBM] * 8,
        (VMEM, VMEM),
        [
            pltpu.VMEM((own, sunlit, lines, LANES), F32),
            pltpu.VMEM((sunlit, lines, LANES), F32),
            pltpu.VMEM((lines, LANES), jnp.int32),
            pltpu.VMEM((lines, LANES), jnp.int32),
            pltpu.VMEM((own, provinces), F32),
            pltpu.SMEM((own,), F32),
            pltpu.SMEM((own,), F32),
            pltpu.SMEM((own,), F32),
            pltpu.SemaphoreType.DMA((own + 7,)),
        ],
        None,
    )(*(pltpu.with_memory_space_constraint(a, pltpu.HBM) for a in inputs))
    all_tracers = lax.all_to_all(weighted, "trc", 0, 0, tiled=True).reshape(tracers, lines, LANES)
    province_part = call(
        province_kernel,
        shape((provinces, own), F32),
        [VMEM] * 6,
        VMEM,
        [
            pltpu.VMEM((provinces, columns), BF16),
            pltpu.VMEM((lines * SUB, LANES), F32),
            pltpu.VMEM((2 * SUB, columns), BF16),
        ],
    )(cot, uptake, nutrient, depth, region, params)
    fed = call(
        feed_kernel,
        shape((tracers, lines, LANES), F32),
        [VMEM, VMEM],
        VMEM,
        [pltpu.VMEM((tracers * lines, LANES), F32), pltpu.VMEM((tracers * lines, LANES), F32)],
    )(uptake_matrix, all_tracers)
    fed = fed.astype(jnp.float16).reshape(sunlit, own, lines, LANES)
    fed = lax.all_to_all(fed, "trc", 0, 0, tiled=True).astype(F32)
    col, halo = call(
        column_kernel,
        (shape((own * lines, levels, LANES), F32), shape((own * lines + 1, levels, LANES), BF16)),
        [VMEM] * 4,
        (VMEM, VMEM),
    )(cot.reshape(-1, LANES), fed.reshape(-1, LANES), depth, params)
    south = lax.ppermute(halo, "tile", up)
    north = lax.ppermute(halo, "tile", down)
    province_part, south, north = lax.optimization_barrier((province_part, south, north))
    own_parts = lax.all_to_all(province_part, "tile", 0, 0, tiled=True)
    tracer_grad = call(
        mixing_kernel,
        shape((own * levels * lines, LANES), F32),
        [VMEM] * 5,
        HBM,
        [
            pltpu.VMEM((levels // SUB, 5, lines // ROWS, SUB, LANES), F32),
            pltpu.VMEM((levels // SUB, 4, lines // ROWS, SUB, LANES), F32),
            pltpu.VMEM((own * levels * lines, LANES), F32),
            pltpu.SemaphoreType.DMA((own,)),
        ],
        pl.CostEstimate(flops=20_000_000, bytes_accessed=100_000_000, transcendentals=0),
    )(col, south, north, depth, params)
    own_parts, tracer_grad = lax.optimization_barrier((own_parts, tracer_grad))
    rate_grad = jnp.sum(own_parts, axis=0, keepdims=True) * (1.0 / (sunlit * columns))
    tracer_grad = tracer_grad.reshape(own, levels, lines, LANES)
    return (undense(tracer_grad, band_rows), rate_grad)


def solution(mesh):
    return jax.shard_map(
        body,
        mesh=mesh,
        in_specs=(
            P("trc", None, "tile", None),
            P("trc", None, "tile", None),
            P(None, "tile", None),
            P("tile", None),
            P("tile", None),
            P(),
            P(None, "trc"),
            P("trc"),
            P("trc"),
            P("trc"),
        ),
        out_specs=(P("trc", None, "tile", None), P("tile", "trc")),
        check_vma=False,
    )
```

```python
import jax
import jax.numpy as jnp
from jax import lax
from jax.experimental import pallas as pl
from jax.experimental.pallas import tpu as pltpu
from jax.sharding import PartitionSpec as P

SCALE = 256.0
LANES = 128
ROWS = 2
SUB = 8
BF16 = jnp.bfloat16
F32 = jnp.float32
VMEM = pl.BlockSpec(memory_space=pltpu.VMEM)
HBM = pl.BlockSpec(memory_space=pltpu.HBM)
PARAMS = pltpu.CompilerParams(vmem_limit_bytes=40 * 1024 * 1024)


def row(ref, *at):
    *lead, r = at
    blocks = ref.shape[-2] // ROWS
    return ref[(*lead, pl.ds(r, blocks, stride=ROWS), slice(None))]


def wet_at(depth, level):
    return (depth > level).astype(F32)


def weighted_kernel(
    cot_hbm, nutrient_hbm, depth_hbm, region_hbm, rates_hbm, half_hbm, sinking_hbm, mixing_hbm,
    out_ref, params_ref, nutrient_ref, depth_ref, region_ref,
    cot_ref, rates_ref, half_ref, sinking_ref, mixing_ref, sems,
):
    own, sunlit = out_ref.shape[1], out_ref.shape[0]
    blocks = cot_ref.shape[2] // ROWS
    pairs = [
        (depth_hbm, depth_ref), (region_hbm, region_ref), (rates_hbm, rates_ref), (nutrient_hbm, nutrient_ref),
        (half_hbm, half_ref), (sinking_hbm, sinking_ref), (mixing_hbm, mixing_ref),
    ]
    pairs += [(cot_hbm.at[t, 0:sunlit], cot_ref.at[t]) for t in range(own)]
    copies = [pltpu.make_async_copy(here, there, sems.at[n]) for n, (here, there) in enumerate(pairs)]
    for copy in copies:
        copy.start()
    for copy in copies[: len(pairs) - own]:
        copy.wait()
    depth = [row(depth_ref, r) for r in range(ROWS)]
    region = [row(region_ref, r) for r in range(ROWS)]
    rest = jnp.zeros((1, LANES - rates_ref.shape[1]), F32)
    for t in range(own):
        line = jnp.concatenate([rates_ref[t : t + 1, :], rest], axis=1)
        line = jnp.broadcast_to(line, (blocks, LANES))
        rates = [jnp.take_along_axis(line, region[r], axis=1) for r in range(ROWS)]
        half = half_ref[t]
        for n, ref in enumerate((half_ref, sinking_ref, mixing_ref)):
            params_ref[n * SUB + t : n * SUB + t + 1, :] = jnp.full((1, LANES), ref[t], F32)
        copies[len(pairs) - own + t].wait()
        for k in range(sunlit):
            rows = []
            for r in range(ROWS):
                food = row(nutrient_ref, k, r)
                limiter = food / (food + half)
                grad = row(cot_ref, t, k, r) * wet_at(depth[r], k)
                rows.append(rates[r] * limiter * grad)
            out_ref[k, t] = jnp.concatenate(rows, axis=0).astype(BF16)


def province_kernel(cot_ref, uptake_ref, nutrient_ref, depth_ref, region_ref, params_ref, out_ref, hot_ref, term_ref, parts_ref):
    provinces, own = out_ref.shape
    sunlit = nutrient_ref.shape[0]
    lines = depth_ref.shape[0]
    depth = depth_ref[...]
    term_ref[...] = jnp.zeros(term_ref.shape, F32)
    for t in range(own):
        half = jnp.broadcast_to(params_ref[t : t + 1, :], (lines, LANES))
        total = jnp.zeros((lines, LANES), F32)
        for k in range(sunlit):
            food = nutrient_ref[k]
            limiter = food / (food + half)
            grad = cot_ref[t, k] * wet_at(depth, k)
            total = total + limiter * uptake_ref[t, k].astype(F32) * grad
        term_ref[pl.ds(t, lines, stride=8), :] = total
    ids = lax.broadcasted_iota(jnp.int32, (provinces, LANES), 0)
    for s in range(lines):
        line = jnp.broadcast_to(region_ref[s : s + 1, :], (provinces, LANES))
        hot_ref[:, s * LANES : (s + 1) * LANES] = (line == ids).astype(F32).astype(BF16)
        term = term_ref[s * 8 : (s + 1) * 8, :]
        high = term.astype(BF16).astype(F32)
        both = jnp.concatenate([high, term - high], axis=0)
        parts_ref[:, s * LANES : (s + 1) * LANES] = both.astype(BF16)
    sums = lax.dot_general(hot_ref[...], parts_ref[...], (((1,), (1,)), ((), ())), preferred_element_type=F32)
    out_ref[...] = sums[:, 0:own] + sums[:, 8 : 8 + own]


def feed_kernel(matrix_ref, weighted_ref, out_ref, wide_ref, fed_ref):
    tracers, lines = weighted_ref.shape[0], weighted_ref.shape[1]
    matrix = matrix_ref[...].astype(F32).T.astype(BF16)
    for t in range(tracers):
        wide_ref[t * lines : (t + 1) * lines, :] = weighted_ref[t].astype(F32)
    for s in range(0, lines, 2):
        cells = [wide_ref[pl.ds(s + i, tracers, stride=lines), :].astype(BF16) for i in range(2)]
        fed = jnp.dot(matrix, jnp.concatenate(cells, axis=1), preferred_element_type=F32) * SCALE
        for i in range(2):
            fed_ref[pl.ds(s + i, tracers, stride=lines), :] = fed[:, i * LANES : (i + 1) * LANES]
    for t in range(tracers):
        out_ref[t] = fed_ref[t * lines : (t + 1) * lines, :]


def column_kernel(cot_ref, fed_ref, depth_ref, params_ref, col_ref, halo_ref):
    lines = depth_ref.shape[0]
    blocks = lines // ROWS
    own = col_ref.shape[0] // lines
    levels = col_ref.shape[1]
    blocks_of = [depth_ref[b * ROWS + r : b * ROWS + r + 1, :] for r in range(ROWS) for b in range(blocks)]
    halo_ref[own * lines] = jnp.concatenate(blocks_of, axis=0).astype(F32).astype(BF16)
    ids = lax.broadcasted_iota(jnp.int32, (SUB, LANES), 0)
    bottom = ids == SUB - 1
    for n in range(lines):
        r, b = n // blocks, n % blocks
        depth = jnp.broadcast_to(blocks_of[n], (SUB, LANES))
        top_wet, low_wet = (depth > ids).astype(F32), (depth > ids + SUB).astype(F32)
        top_next = (depth > ids + 1).astype(F32)
        low_next = jnp.where(bottom, 0.0, (depth > ids + SUB + 1).astype(F32))

        for t in range(own):
            base = (t * levels) * lines + b * ROWS + r
            top = cot_ref[pl.ds(base, SUB, stride=lines), :] * top_wet
            low = cot_ref[pl.ds(base + SUB * lines, SUB, stride=lines), :] * low_wet
            fed = fed_ref[pl.ds(t * lines + n, SUB, stride=own * lines), :] * (1.0 / SCALE)
            top = top + top_wet * fed
            low_up = pltpu.roll(low, SUB - 1, 0)
            top_up = jnp.where(bottom, low_up, pltpu.roll(top, SUB - 1, 0))
            sink = params_ref[SUB + t : SUB + t + 1, :]
            col_top = top + sink * top_next * (top_up - top)
            col_low = low + sink * low_next * (low_up - low)
            both = jnp.concatenate([col_top, col_low], axis=0)
            col_ref[t * lines + n] = both
            halo_ref[t * lines + n] = both.astype(BF16)


def mixing_kernel(col_ref, south_ref, north_ref, depth_ref, params_ref, out_hbm, edges_y_ref, edges_x_ref, out_ref, sems):
    lines = depth_ref.shape[0]
    own = col_ref.shape[0] // lines
    blocks = lines // ROWS
    levels = col_ref.shape[1]
    halves = levels // SUB
    ids = lax.broadcasted_iota(jnp.int32, (SUB, LANES), 0)
    lane_ids = lax.broadcasted_iota(jnp.int32, (SUB, LANES), 1)
    last_lane, first_lane = lane_ids == LANES - 1, lane_ids == 0

    def east(v):
        turned = [pltpu.roll(x, LANES - 1, 1) for x in v]
        return [jnp.where(last_lane, turned[(b + 1) % blocks], turned[b]) for b in range(blocks)]

    def west(v):
        turned = [pltpu.roll(x, 1, 1) for x in v]
        return [jnp.where(first_lane, turned[(b - 1) % blocks], turned[b]) for b in range(blocks)]

    def own_depth(n):
        r, b = n // blocks, n % blocks
        return jnp.broadcast_to(depth_ref[b * ROWS + r : b * ROWS + r + 1, :], (SUB, LANES)).astype(F32)

    def field(which, at, h):
        ref = (south_ref, col_ref, north_ref)[at // ROWS]
        return [ref[which * lines + (at % ROWS) * blocks + b, h * SUB : (h + 1) * SUB, :].astype(F32) for b in range(blocks)]

    far = [ref[own * lines].astype(F32) for ref in (south_ref, north_ref)]
    for h in range(halves):
        at = (ids + h * SUB).astype(F32)
        wet = []
        for i in range(3 * ROWS):
            if i // ROWS == 1:
                depths = [own_depth((i % ROWS) * blocks + b) for b in range(blocks)]
            else:
                band, first = far[i // (2 * ROWS)], (i % ROWS) * blocks
                depths = [jnp.broadcast_to(band[first + b : first + b + 1], (SUB, LANES)) for b in range(blocks)]
            wet.append([(d > at).astype(F32) for d in depths])
        for i in range(3 * ROWS - 1):
            for b in range(blocks):
                edges_y_ref[h, i, b] = wet[i][b] * wet[i + 1][b]
        for i in range(1, 3 * ROWS - 1):
            ahead = east(wet[i])
            for b in range(blocks):
                edges_x_ref[h, i - 1, b] = wet[i][b] * ahead[b]

    def laplacian(rows, h, lo, hi):
        flux = [[edges_y_ref[h, i, b] * (rows[i + 1][b] - rows[i][b]) for b in range(blocks)] for i in range(lo - 1, hi)]
        out = []
        for n, i in enumerate(range(lo, hi)):
            ahead = east(rows[i])
            zonal = [edges_x_ref[h, i - 1, b] * (ahead[b] - rows[i][b]) for b in range(blocks)]
            behind = west(zonal)
            out.append([(flux[n + 1][b] - flux[n][b]) + (zonal[b] - behind[b]) for b in range(blocks)])
        return out

    def copy_out(t):
        part = pl.ds(t * levels * lines, levels * lines)
        return pltpu.make_async_copy(out_ref.at[part], out_hbm.at[part], sems.at[t])

    @pl.loop(0, own)
    def _(t):
        mixing = jnp.broadcast_to(params_ref[pl.ds(2 * SUB + t, 1), :], (SUB, LANES))
        for h in range(halves):
            rows = [field(t, i, h) for i in range(3 * ROWS)]
            once = laplacian(rows, h, 1, 5)
            twice = laplacian([None] + once, h, 2, 4)
            for r in range(ROWS):
                for b in range(blocks):
                    value = rows[ROWS + r][b] - mixing * twice[r][b]
                    out_ref[pl.ds((t * levels + h * SUB) * lines + b * ROWS + r, SUB, stride=lines), :] = value
        copy_out(t).start()

    for t in range(own):
        copy_out(t).wait()


def dense(band):
    *lead, rows, zonal = band.shape
    cut = band.reshape(*lead, rows, zonal // LANES, LANES)
    return jnp.swapaxes(cut, -3, -2).reshape(*lead, rows * zonal // LANES, LANES)


def undense(lines, rows):
    *lead, count, _ = lines.shape
    cut = lines.reshape(*lead, count // rows, rows, LANES)
    return jnp.swapaxes(cut, -3, -2).reshape(*lead, rows, count * LANES // rows)


def call(kernel, shapes, ins, outs, scratch=(), cost=None):
    return pl.pallas_call(
        kernel,
        out_shape=shapes,
        in_specs=ins,
        out_specs=outs,
        scratch_shapes=scratch,
        cost_estimate=cost,
        compiler_params=PARAMS,
    )


def body(
    cotangent,
    uptake_rate,
    nutrient,
    depth_levels,
    region_ids,
    uptake_matrix,
    province_rates,
    half_saturation,
    biharmonic,
    sinking,
):
    own, levels, band_rows, zonal = cotangent.shape
    sunlit = uptake_rate.shape[1]
    columns = band_rows * zonal
    lines = columns // LANES
    provinces = province_rates.shape[0]
    tracers = uptake_matrix.shape[0]
    tiles = lax.axis_size("tile")
    up = [(i, i + 1) for i in range(tiles - 1)]
    down = [(i + 1, i) for i in range(tiles - 1)]
    shape = jax.ShapeDtypeStruct
    cot, uptake, nutrient = dense(cotangent), dense(uptake_rate), dense(nutrient)
    depth, region = dense(depth_levels), dense(region_ids)

    inputs = (cot, nutrient, depth, region, province_rates.T, half_saturation, sinking, biharmonic)
    weighted, params, nutrient, depth, region = call(
        weighted_kernel,
        (
            shape((sunlit, own, lines, LANES), BF16),
            shape((3 * SUB, LANES), F32),
            shape(nutrient.shape, F32),
            shape(depth.shape, jnp.int32),
            shape(region.shape, jnp.int32),
        ),
        [HBM] * 8,
        (VMEM,) * 5,
        [
            pltpu.VMEM((own, sunlit, lines, LANES), F32),
            pltpu.VMEM((own, provinces), F32),
            pltpu.SMEM((own,), F32),
            pltpu.SMEM((own,), F32),
            pltpu.SMEM((own,), F32),
            pltpu.SemaphoreType.DMA((own + 7,)),
        ],
        None,
    )(*(pltpu.with_memory_space_constraint(a, pltpu.HBM) for a in inputs))
    all_tracers = lax.all_to_all(weighted, "trc", 0, 0, tiled=True).reshape(tracers, lines, LANES)
    province_part = call(
        province_kernel,
        shape((provinces, own), F32),
        [VMEM] * 6,
        VMEM,
        [
            pltpu.VMEM((provinces, columns), BF16),
            pltpu.VMEM((lines * SUB, LANES), F32),
            pltpu.VMEM((2 * SUB, columns), BF16),
        ],
    )(cot, uptake, nutrient, depth, region, params)
    fed = call(
        feed_kernel,
        shape((tracers, lines, LANES), F32),
        [VMEM, VMEM],
        VMEM,
        [pltpu.VMEM((tracers * lines, LANES), F32), pltpu.VMEM((tracers * lines, LANES), F32)],
    )(uptake_matrix, all_tracers)
    fed = fed.astype(jnp.float16).reshape(sunlit, own, lines, LANES)
    fed = lax.all_to_all(fed, "trc", 0, 0, tiled=True)
    fed, province_part = lax.optimization_barrier((fed, province_part))
    fed = fed.astype(F32)
    col, halo = call(
        column_kernel,
        (shape((own * lines, levels, LANES), F32), shape((own * lines + 1, levels, LANES), BF16)),
        [VMEM] * 4,
        (VMEM, VMEM),
    )(cot.reshape(-1, LANES), fed.reshape(-1, LANES), depth, params)
    south = lax.ppermute(halo, "tile", up)
    north = lax.ppermute(halo, "tile", down)
    own_parts = lax.all_to_all(province_part, "tile", 0, 0, tiled=True)
    tracer_grad = call(
        mixing_kernel,
        shape((own * levels * lines, LANES), F32),
        [VMEM] * 5,
        HBM,
        [
            pltpu.VMEM((levels // SUB, 5, lines // ROWS, SUB, LANES), F32),
            pltpu.VMEM((levels // SUB, 4, lines // ROWS, SUB, LANES), F32),
            pltpu.VMEM((own * levels * lines, LANES), F32),
            pltpu.SemaphoreType.DMA((own,)),
        ],
        pl.CostEstimate(flops=20_000_000, bytes_accessed=100_000_000, transcendentals=0),
    )(col, south, north, depth, params)
    own_parts, tracer_grad = lax.optimization_barrier((own_parts, tracer_grad))
    rate_grad = jnp.sum(own_parts, axis=0, keepdims=True) * (1.0 / (sunlit * columns))
    tracer_grad = tracer_grad.reshape(own, levels, lines, LANES)
    return (undense(tracer_grad, band_rows), rate_grad)


def solution(mesh):
    return jax.shard_map(
        body,
        mesh=mesh,
        in_specs=(
            P("trc", None, "tile", None),
            P("trc", None, "tile", None),
            P(None, "tile", None),
            P("tile", None),
            P("tile", None),
            P(),
            P(None, "trc"),
            P("trc"),
            P("trc"),
            P("trc"),
        ),
        out_specs=(P("trc", None, "tile", None), P("tile", "trc")),
        check_vma=False,
    )
```

```python
import jax
import jax.numpy as jnp
from jax import lax
from jax.experimental import pallas as pl
from jax.experimental.pallas import tpu as pltpu
from jax.sharding import PartitionSpec as P

SCALE = 256.0
LANES = 128
ROWS = 2
SUB = 8
BF16 = jnp.bfloat16
F32 = jnp.float32
VMEM = pl.BlockSpec(memory_space=pltpu.VMEM)
HBM = pl.BlockSpec(memory_space=pltpu.HBM)
PARAMS = pltpu.CompilerParams(vmem_limit_bytes=40 * 1024 * 1024)


def row(ref, *at):
    *lead, r = at
    blocks = ref.shape[-2] // ROWS
    return ref[(*lead, pl.ds(r, blocks, stride=ROWS), slice(None))]


def wet_at(depth, level):
    return (depth > level).astype(F32)


def weighted_kernel(
    cot_hbm, nutrient_hbm, depth_hbm, region_hbm, rates_hbm, half_hbm, sinking_hbm, mixing_hbm,
    out_ref, params_ref, nutrient_ref, depth_ref, region_ref,
    cot_ref, rates_ref, half_ref, sinking_ref, mixing_ref, sems,
):
    own, sunlit = out_ref.shape[1], out_ref.shape[0]
    blocks = cot_ref.shape[2] // ROWS
    pairs = [
        (depth_hbm, depth_ref), (region_hbm, region_ref), (rates_hbm, rates_ref), (nutrient_hbm, nutrient_ref),
        (half_hbm, half_ref), (sinking_hbm, sinking_ref), (mixing_hbm, mixing_ref),
    ]
    pairs += [(cot_hbm.at[t, 0:sunlit], cot_ref.at[t]) for t in range(own)]
    copies = [pltpu.make_async_copy(here, there, sems.at[n]) for n, (here, there) in enumerate(pairs)]
    for copy in copies:
        copy.start()
    for copy in copies[: len(pairs) - own]:
        copy.wait()
    depth = [row(depth_ref, r) for r in range(ROWS)]
    region = [row(region_ref, r) for r in range(ROWS)]
    rest = jnp.zeros((1, LANES - rates_ref.shape[1]), F32)
    for t in range(own):
        line = jnp.concatenate([rates_ref[t : t + 1, :], rest], axis=1)
        line = jnp.broadcast_to(line, (blocks, LANES))
        rates = [jnp.take_along_axis(line, region[r], axis=1) for r in range(ROWS)]
        half = half_ref[t]
        for n, ref in enumerate((half_ref, sinking_ref, mixing_ref)):
            params_ref[n * SUB + t : n * SUB + t + 1, :] = jnp.full((1, LANES), ref[t], F32)
        copies[len(pairs) - own + t].wait()
        for k in range(sunlit):
            rows = []
            for r in range(ROWS):
                food = row(nutrient_ref, k, r)
                limiter = food / (food + half)
                grad = row(cot_ref, t, k, r) * wet_at(depth[r], k)
                rows.append(rates[r] * limiter * grad)
            out_ref[k, t] = jnp.concatenate(rows, axis=0).astype(BF16)


def province_kernel(cot_ref, uptake_ref, nutrient_ref, depth_ref, region_ref, params_ref, out_ref, hot_ref, term_ref, parts_ref):
    provinces, own = out_ref.shape
    sunlit = nutrient_ref.shape[0]
    lines = depth_ref.shape[0]
    depth = depth_ref[...]
    term_ref[...] = jnp.zeros(term_ref.shape, F32)
    for t in range(own):
        half = jnp.broadcast_to(params_ref[t : t + 1, :], (lines, LANES))
        total = jnp.zeros((lines, LANES), F32)
        for k in range(sunlit):
            food = nutrient_ref[k]
            limiter = food / (food + half)
            grad = cot_ref[t, k] * wet_at(depth, k)
            total = total + limiter * uptake_ref[t, k].astype(F32) * grad
        term_ref[pl.ds(t, lines, stride=8), :] = total
    ids = lax.broadcasted_iota(jnp.int32, (provinces, LANES), 0)
    for s in range(lines):
        line = jnp.broadcast_to(region_ref[s : s + 1, :], (provinces, LANES))
        hot_ref[:, s * LANES : (s + 1) * LANES] = (line == ids).astype(F32).astype(BF16)
        term = term_ref[s * 8 : (s + 1) * 8, :]
        high = term.astype(BF16).astype(F32)
        both = jnp.concatenate([high, term - high], axis=0)
        parts_ref[:, s * LANES : (s + 1) * LANES] = both.astype(BF16)
    sums = lax.dot_general(hot_ref[...], parts_ref[...], (((1,), (1,)), ((), ())), preferred_element_type=F32)
    scale = 1.0 / (sunlit * lines * LANES)
    out_ref[...] = (sums[:, 0:own] + sums[:, SUB : SUB + own]) * scale


def feed_kernel(matrix_ref, weighted_ref, out_ref, wide_ref, fed_ref):
    tracers, lines = weighted_ref.shape[0], weighted_ref.shape[1]
    matrix = matrix_ref[...].astype(F32).T.astype(BF16)
    for t in range(tracers):
        wide_ref[t * lines : (t + 1) * lines, :] = weighted_ref[t].astype(F32)
    for s in range(0, lines, 2):
        cells = [wide_ref[pl.ds(s + i, tracers, stride=lines), :].astype(BF16) for i in range(2)]
        fed = jnp.dot(matrix, jnp.concatenate(cells, axis=1), preferred_element_type=F32) * SCALE
        for i in range(2):
            fed_ref[pl.ds(s + i, tracers, stride=lines), :] = fed[:, i * LANES : (i + 1) * LANES]
    for t in range(tracers):
        out_ref[t] = fed_ref[t * lines : (t + 1) * lines, :]


def column_kernel(cot_ref, fed_ref, depth_ref, params_ref, part_ref, other_ref, col_ref, halo_ref, pair_ref):
    pair_ref[...] = part_ref[...] + other_ref[...]
    lines = depth_ref.shape[0]
    blocks = lines // ROWS
    own = col_ref.shape[0] // lines
    levels = col_ref.shape[1]
    blocks_of = [depth_ref[b * ROWS + r : b * ROWS + r + 1, :] for r in range(ROWS) for b in range(blocks)]
    halo_ref[own * lines] = jnp.concatenate(blocks_of, axis=0).astype(F32).astype(BF16)
    ids = lax.broadcasted_iota(jnp.int32, (SUB, LANES), 0)
    bottom = ids == SUB - 1
    for n in range(lines):
        r, b = n // blocks, n % blocks
        depth = jnp.broadcast_to(blocks_of[n], (SUB, LANES))
        top_wet, low_wet = (depth > ids).astype(F32), (depth > ids + SUB).astype(F32)
        top_next = (depth > ids + 1).astype(F32)
        low_next = jnp.where(bottom, 0.0, (depth > ids + SUB + 1).astype(F32))

        for t in range(own):
            base = (t * levels) * lines + b * ROWS + r
            top = cot_ref[pl.ds(base, SUB, stride=lines), :] * top_wet
            low = cot_ref[pl.ds(base + SUB * lines, SUB, stride=lines), :] * low_wet
            fed = fed_ref[pl.ds(t * lines + n, SUB, stride=own * lines), :] * (1.0 / SCALE)
            top = top + top_wet * fed
            low_up = pltpu.roll(low, SUB - 1, 0)
            top_up = jnp.where(bottom, low_up, pltpu.roll(top, SUB - 1, 0))
            sink = params_ref[SUB + t : SUB + t + 1, :]
            col_top = top + sink * top_next * (top_up - top)
            col_low = low + sink * low_next * (low_up - low)
            both = jnp.concatenate([col_top, col_low], axis=0)
            col_ref[t * lines + n] = both
            halo_ref[t * lines + n] = both.astype(BF16)


def mixing_kernel(col_ref, south_ref, north_ref, depth_ref, params_ref, out_hbm, edges_y_ref, edges_x_ref, out_ref, sems):
    lines = depth_ref.shape[0]
    own = col_ref.shape[0] // lines
    blocks = lines // ROWS
    levels = col_ref.shape[1]
    halves = levels // SUB
    ids = lax.broadcasted_iota(jnp.int32, (SUB, LANES), 0)
    lane_ids = lax.broadcasted_iota(jnp.int32, (SUB, LANES), 1)
    last_lane, first_lane = lane_ids == LANES - 1, lane_ids == 0

    def east(v):
        turned = [pltpu.roll(x, LANES - 1, 1) for x in v]
        return [jnp.where(last_lane, turned[(b + 1) % blocks], turned[b]) for b in range(blocks)]

    def west(v):
        turned = [pltpu.roll(x, 1, 1) for x in v]
        return [jnp.where(first_lane, turned[(b - 1) % blocks], turned[b]) for b in range(blocks)]

    def own_depth(n):
        r, b = n // blocks, n % blocks
        return jnp.broadcast_to(depth_ref[b * ROWS + r : b * ROWS + r + 1, :], (SUB, LANES)).astype(F32)

    def field(which, at, h):
        ref = (south_ref, col_ref, north_ref)[at // ROWS]
        return [ref[which * lines + (at % ROWS) * blocks + b, h * SUB : (h + 1) * SUB, :].astype(F32) for b in range(blocks)]

    far = [ref[own * lines].astype(F32) for ref in (south_ref, north_ref)]
    for h in range(halves):
        at = (ids + h * SUB).astype(F32)
        wet = []
        for i in range(3 * ROWS):
            if i // ROWS == 1:
                depths = [own_depth((i % ROWS) * blocks + b) for b in range(blocks)]
            else:
                band, first = far[i // (2 * ROWS)], (i % ROWS) * blocks
                depths = [jnp.broadcast_to(band[first + b : first + b + 1], (SUB, LANES)) for b in range(blocks)]
            wet.append([(d > at).astype(F32) for d in depths])
        for i in range(3 * ROWS - 1):
            for b in range(blocks):
                edges_y_ref[h, i, b] = wet[i][b] * wet[i + 1][b]
        for i in range(1, 3 * ROWS - 1):
            ahead = east(wet[i])
            for b in range(blocks):
                edges_x_ref[h, i - 1, b] = wet[i][b] * ahead[b]

    def laplacian(rows, h, lo, hi):
        flux = [[edges_y_ref[h, i, b] * (rows[i + 1][b] - rows[i][b]) for b in range(blocks)] for i in range(lo - 1, hi)]
        out = []
        for n, i in enumerate(range(lo, hi)):
            ahead = east(rows[i])
            zonal = [edges_x_ref[h, i - 1, b] * (ahead[b] - rows[i][b]) for b in range(blocks)]
            behind = west(zonal)
            out.append([(flux[n + 1][b] - flux[n][b]) + (zonal[b] - behind[b]) for b in range(blocks)])
        return out

    def copy_out(t):
        part = pl.ds(t * levels * lines, levels * lines)
        return pltpu.make_async_copy(out_ref.at[part], out_hbm.at[part], sems.at[t])

    @pl.loop(0, own)
    def _(t):
        mixing = jnp.broadcast_to(params_ref[pl.ds(2 * SUB + t, 1), :], (SUB, LANES))
        for h in range(halves):
            rows = [field(t, i, h) for i in range(3 * ROWS)]
            once = laplacian(rows, h, 1, 5)
            twice = laplacian([None] + once, h, 2, 4)
            for r in range(ROWS):
                for b in range(blocks):
                    value = rows[ROWS + r][b] - mixing * twice[r][b]
                    out_ref[pl.ds((t * levels + h * SUB) * lines + b * ROWS + r, SUB, stride=lines), :] = value
        copy_out(t).start()

    for t in range(own):
        copy_out(t).wait()


def dense(band):
    *lead, rows, zonal = band.shape
    cut = band.reshape(*lead, rows, zonal // LANES, LANES)
    return jnp.swapaxes(cut, -3, -2).reshape(*lead, rows * zonal // LANES, LANES)


def undense(lines, rows):
    *lead, count, _ = lines.shape
    cut = lines.reshape(*lead, count // rows, rows, LANES)
    return jnp.swapaxes(cut, -3, -2).reshape(*lead, rows, count * LANES // rows)


def call(kernel, shapes, ins, outs, scratch=(), cost=None):
    return pl.pallas_call(
        kernel,
        out_shape=shapes,
        in_specs=ins,
        out_specs=outs,
        scratch_shapes=scratch,
        cost_estimate=cost,
        compiler_params=PARAMS,
    )


def body(
    cotangent,
    uptake_rate,
    nutrient,
    depth_levels,
    region_ids,
    uptake_matrix,
    province_rates,
    half_saturation,
    biharmonic,
    sinking,
):
    own, levels, band_rows, zonal = cotangent.shape
    sunlit = uptake_rate.shape[1]
    columns = band_rows * zonal
    lines = columns // LANES
    provinces = province_rates.shape[0]
    tracers = uptake_matrix.shape[0]
    tiles = lax.axis_size("tile")
    up = [(i, i + 1) for i in range(tiles - 1)]
    down = [(i + 1, i) for i in range(tiles - 1)]
    shape = jax.ShapeDtypeStruct
    cot, uptake, nutrient = dense(cotangent), dense(uptake_rate), dense(nutrient)
    depth, region = dense(depth_levels), dense(region_ids)

    inputs = (cot, nutrient, depth, region, province_rates.T, half_saturation, sinking, biharmonic)
    weighted, params, nutrient, depth, region = call(
        weighted_kernel,
        (
            shape((sunlit, own, lines, LANES), BF16),
            shape((3 * SUB, LANES), F32),
            shape(nutrient.shape, F32),
            shape(depth.shape, jnp.int32),
            shape(region.shape, jnp.int32),
        ),
        [HBM] * 8,
        (VMEM,) * 5,
        [
            pltpu.VMEM((own, sunlit, lines, LANES), F32),
            pltpu.VMEM((own, provinces), F32),
            pltpu.SMEM((own,), F32),
            pltpu.SMEM((own,), F32),
            pltpu.SMEM((own,), F32),
            pltpu.SemaphoreType.DMA((own + 7,)),
        ],
        None,
    )(*(pltpu.with_memory_space_constraint(a, pltpu.HBM) for a in inputs))
    all_tracers = lax.all_to_all(weighted, "trc", 0, 0, tiled=True).reshape(tracers, lines, LANES)
    province_part = call(
        province_kernel,
        shape((provinces, own), F32),
        [VMEM] * 6,
        VMEM,
        [
            pltpu.VMEM((provinces, columns), BF16),
            pltpu.VMEM((lines * SUB, LANES), F32),
            pltpu.VMEM((2 * SUB, columns), BF16),
        ],
    )(cot, uptake, nutrient, depth, region, params)
    all_tracers, province_part = lax.optimization_barrier((all_tracers, province_part))
    other_part = lax.ppermute(province_part, "tile", [(i, i ^ 1) for i in range(tiles)])
    fed = call(
        feed_kernel,
        shape((tracers, lines, LANES), F32),
        [VMEM, VMEM],
        VMEM,
        [pltpu.VMEM((tracers * lines, LANES), F32), pltpu.VMEM((tracers * lines, LANES), F32)],
    )(uptake_matrix, all_tracers)
    fed = fed.astype(jnp.float16).reshape(sunlit, own, lines, LANES)
    fed = lax.all_to_all(fed, "trc", 0, 0, tiled=True)
    fed = fed.astype(F32)
    col, halo, pair_part = call(
        column_kernel,
        (
            shape((own * lines, levels, LANES), F32),
            shape((own * lines + 1, levels, LANES), BF16),
            shape(province_part.shape, F32),
        ),
        [VMEM] * 6,
        (VMEM,) * 3,
    )(cot.reshape(-1, LANES), fed.reshape(-1, LANES), depth, params, province_part, other_part)
    south = lax.ppermute(halo, "tile", up)
    north = lax.ppermute(halo, "tile", down)
    groups = [list(range(core, tiles, 2)) for core in range(2)]
    own_parts = lax.all_to_all(pair_part, "tile", 0, 0, axis_index_groups=groups, tiled=True)
    tracer_grad = call(
        mixing_kernel,
        shape((own * levels * lines, LANES), F32),
        [VMEM] * 5,
        HBM,
        [
            pltpu.VMEM((levels // SUB, 5, lines // ROWS, SUB, LANES), F32),
            pltpu.VMEM((levels // SUB, 4, lines // ROWS, SUB, LANES), F32),
            pltpu.VMEM((own * levels * lines, LANES), F32),
            pltpu.SemaphoreType.DMA((own,)),
        ],
        pl.CostEstimate(flops=1_000_000, bytes_accessed=2_000_000, transcendentals=0),
    )(col, south, north, depth, params)
    own_parts, tracer_grad = lax.optimization_barrier((own_parts, tracer_grad))
    both = jnp.sum(own_parts.reshape(tiles // 2, 2, own), axis=0)
    rate_grad = jnp.where((lax.axis_index("tile") & 1) == 0, both[0:1], both[1:2])
    tracer_grad = tracer_grad.reshape(own, levels, lines, LANES)
    return (undense(tracer_grad, band_rows), rate_grad)


def solution(mesh):
    return jax.shard_map(
        body,
        mesh=mesh,
        in_specs=(
            P("trc", None, "tile", None),
            P("trc", None, "tile", None),
            P(None, "tile", None),
            P("tile", None),
            P("tile", None),
            P(),
            P(None, "trc"),
            P("trc"),
            P("trc"),
            P("trc"),
        ),
        out_specs=(P("trc", None, "tile", None), P("tile", "trc")),
        check_vma=False,
    )
```

```python
import jax
import jax.numpy as jnp
from jax import lax
from jax.experimental import pallas as pl
from jax.experimental.pallas import tpu as pltpu
from jax.sharding import PartitionSpec as P

SCALE = 256.0
LANES = 128
ROWS = 2
SUB = 8
CHIPS_X, CHIPS_Z, CORES = 4, 8, 2
BF16 = jnp.bfloat16
F32 = jnp.float32
VMEM = pl.BlockSpec(memory_space=pltpu.VMEM)
HBM = pl.BlockSpec(memory_space=pltpu.HBM)
PARAMS = pltpu.CompilerParams(vmem_limit_bytes=40 * 1024 * 1024)


def row(ref, *at):
    *lead, r = at
    blocks = ref.shape[-2] // ROWS
    return ref[(*lead, pl.ds(r, blocks, stride=ROWS), slice(None))]


def wet_at(depth, level):
    return (depth > level).astype(F32)


def weighted_kernel(
    cot_hbm, nutrient_hbm, depth_hbm, region_hbm, rates_hbm, half_hbm, sinking_hbm, mixing_hbm,
    out_ref, params_ref, nutrient_ref, depth_ref, region_ref,
    cot_ref, rates_ref, half_ref, sinking_ref, mixing_ref, sems,
):
    own, sunlit = out_ref.shape[1], out_ref.shape[0]
    blocks = cot_ref.shape[2] // ROWS
    pairs = [
        (depth_hbm, depth_ref), (region_hbm, region_ref), (rates_hbm, rates_ref), (nutrient_hbm, nutrient_ref),
        (half_hbm, half_ref), (sinking_hbm, sinking_ref), (mixing_hbm, mixing_ref),
    ]
    pairs += [(cot_hbm.at[t, 0:sunlit], cot_ref.at[t]) for t in range(own)]
    copies = [pltpu.make_async_copy(here, there, sems.at[n]) for n, (here, there) in enumerate(pairs)]
    for copy in copies:
        copy.start()
    for copy in copies[: len(pairs) - own]:
        copy.wait()
    depth = [row(depth_ref, r) for r in range(ROWS)]
    region = [row(region_ref, r) for r in range(ROWS)]
    rest = jnp.zeros((1, LANES - rates_ref.shape[1]), F32)
    for t in range(own):
        line = jnp.concatenate([rates_ref[t : t + 1, :], rest], axis=1)
        line = jnp.broadcast_to(line, (blocks, LANES))
        rates = [jnp.take_along_axis(line, region[r], axis=1) for r in range(ROWS)]
        half = half_ref[t]
        for n, ref in enumerate((half_ref, sinking_ref, mixing_ref)):
            params_ref[n * SUB + t : n * SUB + t + 1, :] = jnp.full((1, LANES), ref[t], F32)
        copies[len(pairs) - own + t].wait()
        for k in range(sunlit):
            rows = []
            for r in range(ROWS):
                food = row(nutrient_ref, k, r)
                limiter = food / (food + half)
                grad = row(cot_ref, t, k, r) * wet_at(depth[r], k)
                rows.append(rates[r] * limiter * grad)
            out_ref[k, t] = jnp.concatenate(rows, axis=0).astype(BF16)


def province_kernel(cot_ref, uptake_ref, nutrient_ref, depth_ref, region_ref, params_ref, out_ref, hot_ref, term_ref, parts_ref):
    provinces, own = out_ref.shape
    sunlit = nutrient_ref.shape[0]
    lines = depth_ref.shape[0]
    depth = depth_ref[...]
    term_ref[...] = jnp.zeros(term_ref.shape, F32)
    for t in range(own):
        half = jnp.broadcast_to(params_ref[t : t + 1, :], (lines, LANES))
        total = jnp.zeros((lines, LANES), F32)
        for k in range(sunlit):
            food = nutrient_ref[k]
            limiter = food / (food + half)
            grad = cot_ref[t, k] * wet_at(depth, k)
            total = total + limiter * uptake_ref[t, k].astype(F32) * grad
        term_ref[pl.ds(t, lines, stride=8), :] = total
    place = lax.broadcasted_iota(jnp.int32, (provinces, LANES), 0)
    z, x, core = place // (CHIPS_X * CORES), (place // CORES) % CHIPS_X, place % CORES
    ids = (x * CHIPS_Z + z) * CORES + core
    for s in range(lines):
        line = jnp.broadcast_to(region_ref[s : s + 1, :], (provinces, LANES))
        hot_ref[:, s * LANES : (s + 1) * LANES] = (line == ids).astype(F32).astype(BF16)
        term = term_ref[s * 8 : (s + 1) * 8, :]
        high = term.astype(BF16).astype(F32)
        both = jnp.concatenate([high, term - high], axis=0)
        parts_ref[:, s * LANES : (s + 1) * LANES] = both.astype(BF16)
    sums = lax.dot_general(hot_ref[...], parts_ref[...], (((1,), (1,)), ((), ())), preferred_element_type=F32)
    scale = 1.0 / (sunlit * lines * LANES)
    out_ref[...] = (sums[:, 0:own] + sums[:, SUB : SUB + own]) * scale


def feed_kernel(matrix_ref, weighted_ref, out_ref, wide_ref, fed_ref):
    tracers, lines = weighted_ref.shape[0], weighted_ref.shape[1]
    matrix = matrix_ref[...].astype(F32).T.astype(BF16)
    for t in range(tracers):
        wide_ref[t * lines : (t + 1) * lines, :] = weighted_ref[t].astype(F32)
    for s in range(0, lines, 2):
        cells = [wide_ref[pl.ds(s + i, tracers, stride=lines), :].astype(BF16) for i in range(2)]
        fed = jnp.dot(matrix, jnp.concatenate(cells, axis=1), preferred_element_type=F32) * SCALE
        for i in range(2):
            fed_ref[pl.ds(s + i, tracers, stride=lines), :] = fed[:, i * LANES : (i + 1) * LANES]
    for t in range(tracers):
        out_ref[t] = fed_ref[t * lines : (t + 1) * lines, :]


def column_kernel(cot_ref, fed_ref, depth_ref, params_ref, col_ref, halo_ref):
    lines = depth_ref.shape[0]
    blocks = lines // ROWS
    own = col_ref.shape[0] // lines
    levels = col_ref.shape[1]
    blocks_of = [depth_ref[b * ROWS + r : b * ROWS + r + 1, :] for r in range(ROWS) for b in range(blocks)]
    halo_ref[own * lines] = jnp.concatenate(blocks_of, axis=0).astype(F32).astype(BF16)
    ids = lax.broadcasted_iota(jnp.int32, (SUB, LANES), 0)
    bottom = ids == SUB - 1
    for n in range(lines):
        r, b = n // blocks, n % blocks
        depth = jnp.broadcast_to(blocks_of[n], (SUB, LANES))
        top_wet, low_wet = (depth > ids).astype(F32), (depth > ids + SUB).astype(F32)
        top_next = (depth > ids + 1).astype(F32)
        low_next = jnp.where(bottom, 0.0, (depth > ids + SUB + 1).astype(F32))

        for t in range(own):
            base = (t * levels) * lines + b * ROWS + r
            top = cot_ref[pl.ds(base, SUB, stride=lines), :] * top_wet
            low = cot_ref[pl.ds(base + SUB * lines, SUB, stride=lines), :] * low_wet
            fed = fed_ref[pl.ds(t * lines + n, SUB, stride=own * lines), :] * (1.0 / SCALE)
            top = top + top_wet * fed
            low_up = pltpu.roll(low, SUB - 1, 0)
            top_up = jnp.where(bottom, low_up, pltpu.roll(top, SUB - 1, 0))
            sink = params_ref[SUB + t : SUB + t + 1, :]
            col_top = top + sink * top_next * (top_up - top)
            col_low = low + sink * low_next * (low_up - low)
            both = jnp.concatenate([col_top, col_low], axis=0)
            col_ref[t * lines + n] = both
            halo_ref[t * lines + n] = both.astype(BF16)


def mixing_kernel(col_ref, south_ref, north_ref, depth_ref, params_ref, out_hbm, edges_y_ref, edges_x_ref, out_ref, sems):
    lines = depth_ref.shape[0]
    own = col_ref.shape[0] // lines
    blocks = lines // ROWS
    levels = col_ref.shape[1]
    halves = levels // SUB
    ids = lax.broadcasted_iota(jnp.int32, (SUB, LANES), 0)
    lane_ids = lax.broadcasted_iota(jnp.int32, (SUB, LANES), 1)
    last_lane, first_lane = lane_ids == LANES - 1, lane_ids == 0

    def east(v):
        turned = [pltpu.roll(x, LANES - 1, 1) for x in v]
        return [jnp.where(last_lane, turned[(b + 1) % blocks], turned[b]) for b in range(blocks)]

    def west(v):
        turned = [pltpu.roll(x, 1, 1) for x in v]
        return [jnp.where(first_lane, turned[(b - 1) % blocks], turned[b]) for b in range(blocks)]

    def own_depth(n):
        r, b = n // blocks, n % blocks
        return jnp.broadcast_to(depth_ref[b * ROWS + r : b * ROWS + r + 1, :], (SUB, LANES)).astype(F32)

    def field(which, at, h):
        ref = (south_ref, col_ref, north_ref)[at // ROWS]
        return [ref[which * lines + (at % ROWS) * blocks + b, h * SUB : (h + 1) * SUB, :].astype(F32) for b in range(blocks)]

    far = [ref[own * lines].astype(F32) for ref in (south_ref, north_ref)]
    for h in range(halves):
        at = (ids + h * SUB).astype(F32)
        wet = []
        for i in range(3 * ROWS):
            if i // ROWS == 1:
                depths = [own_depth((i % ROWS) * blocks + b) for b in range(blocks)]
            else:
                band, first = far[i // (2 * ROWS)], (i % ROWS) * blocks
                depths = [jnp.broadcast_to(band[first + b : first + b + 1], (SUB, LANES)) for b in range(blocks)]
            wet.append([(d > at).astype(F32) for d in depths])
        for i in range(3 * ROWS - 1):
            for b in range(blocks):
                edges_y_ref[h, i, b] = wet[i][b] * wet[i + 1][b]
        for i in range(1, 3 * ROWS - 1):
            ahead = east(wet[i])
            for b in range(blocks):
                edges_x_ref[h, i - 1, b] = wet[i][b] * ahead[b]

    def laplacian(rows, h, lo, hi):
        flux = [[edges_y_ref[h, i, b] * (rows[i + 1][b] - rows[i][b]) for b in range(blocks)] for i in range(lo - 1, hi)]
        out = []
        for n, i in enumerate(range(lo, hi)):
            ahead = east(rows[i])
            zonal = [edges_x_ref[h, i - 1, b] * (ahead[b] - rows[i][b]) for b in range(blocks)]
            behind = west(zonal)
            out.append([(flux[n + 1][b] - flux[n][b]) + (zonal[b] - behind[b]) for b in range(blocks)])
        return out

    def copy_out(t):
        part = pl.ds(t * levels * lines, levels * lines)
        return pltpu.make_async_copy(out_ref.at[part], out_hbm.at[part], sems.at[t])

    @pl.loop(0, own)
    def _(t):
        mixing = jnp.broadcast_to(params_ref[pl.ds(2 * SUB + t, 1), :], (SUB, LANES))
        for h in range(halves):
            rows = [field(t, i, h) for i in range(3 * ROWS)]
            once = laplacian(rows, h, 1, 5)
            twice = laplacian([None] + once, h, 2, 4)
            for r in range(ROWS):
                for b in range(blocks):
                    value = rows[ROWS + r][b] - mixing * twice[r][b]
                    out_ref[pl.ds((t * levels + h * SUB) * lines + b * ROWS + r, SUB, stride=lines), :] = value
        copy_out(t).start()

    for t in range(own):
        copy_out(t).wait()


def dense(band):
    *lead, rows, zonal = band.shape
    cut = band.reshape(*lead, rows, zonal // LANES, LANES)
    return jnp.swapaxes(cut, -3, -2).reshape(*lead, rows * zonal // LANES, LANES)


def undense(lines, rows):
    *lead, count, _ = lines.shape
    cut = lines.reshape(*lead, count // rows, rows, LANES)
    return jnp.swapaxes(cut, -3, -2).reshape(*lead, rows, count * LANES // rows)


def call(kernel, shapes, ins, outs, scratch=(), cost=None):
    return pl.pallas_call(
        kernel,
        out_shape=shapes,
        in_specs=ins,
        out_specs=outs,
        scratch_shapes=scratch,
        cost_estimate=cost,
        compiler_params=PARAMS,
    )


def body(
    cotangent,
    uptake_rate,
    nutrient,
    depth_levels,
    region_ids,
    uptake_matrix,
    province_rates,
    half_saturation,
    biharmonic,
    sinking,
):
    own, levels, band_rows, zonal = cotangent.shape
    sunlit = uptake_rate.shape[1]
    columns = band_rows * zonal
    lines = columns // LANES
    provinces = province_rates.shape[0]
    tracers = uptake_matrix.shape[0]
    tiles = lax.axis_size("tile")
    up = [(i, i + 1) for i in range(tiles - 1)]
    down = [(i + 1, i) for i in range(tiles - 1)]
    shape = jax.ShapeDtypeStruct
    cot, uptake, nutrient = dense(cotangent), dense(uptake_rate), dense(nutrient)
    depth, region = dense(depth_levels), dense(region_ids)

    inputs = (cot, nutrient, depth, region, province_rates.T, half_saturation, sinking, biharmonic)
    weighted, params, nutrient, depth, region = call(
        weighted_kernel,
        (
            shape((sunlit, own, lines, LANES), BF16),
            shape((3 * SUB, LANES), F32),
            shape(nutrient.shape, F32),
            shape(depth.shape, jnp.int32),
            shape(region.shape, jnp.int32),
        ),
        [HBM] * 8,
        (VMEM,) * 5,
        [
            pltpu.VMEM((own, sunlit, lines, LANES), F32),
            pltpu.VMEM((own, provinces), F32),
            pltpu.SMEM((own,), F32),
            pltpu.SMEM((own,), F32),
            pltpu.SMEM((own,), F32),
            pltpu.SemaphoreType.DMA((own + 7,)),
        ],
        None,
    )(*(pltpu.with_memory_space_constraint(a, pltpu.HBM) for a in inputs))
    all_tracers = lax.all_to_all(weighted, "trc", 0, 0, tiled=True).reshape(tracers, lines, LANES)
    province_part = call(
        province_kernel,
        shape((provinces, own), F32),
        [VMEM] * 6,
        VMEM,
        [
            pltpu.VMEM((provinces, columns), BF16),
            pltpu.VMEM((lines * SUB, LANES), F32),
            pltpu.VMEM((2 * SUB, columns), BF16),
        ],
    )(cot, uptake, nutrient, depth, region, params)
    def exchanged(part, step):
        return part + lax.ppermute(part, "tile", [(i, i ^ step) for i in range(tiles)])

    chip_sum = exchanged(province_part, 1)
    half_sum = exchanged(chip_sum, CHIPS_Z * CORES)
    all_tracers, _ = lax.optimization_barrier((all_tracers, half_sum))
    line_sum = exchanged(half_sum, 2 * CHIPS_Z * CORES)
    fed = call(
        feed_kernel,
        shape((tracers, lines, LANES), F32),
        [VMEM, VMEM],
        VMEM,
        [pltpu.VMEM((tracers * lines, LANES), F32), pltpu.VMEM((tracers * lines, LANES), F32)],
    )(uptake_matrix, all_tracers)
    fed = fed.astype(jnp.float16).reshape(sunlit, own, lines, LANES)
    fed = lax.all_to_all(fed, "trc", 0, 0, tiled=True)
    fed, _ = lax.optimization_barrier((fed, line_sum))
    fed = fed.astype(F32)
    col, halo = call(
        column_kernel,
        (shape((own * lines, levels, LANES), F32), shape((own * lines + 1, levels, LANES), BF16)),
        [VMEM] * 4,
        (VMEM, VMEM),
    )(cot.reshape(-1, LANES), fed.reshape(-1, LANES), depth, params)
    south = lax.ppermute(halo, "tile", up)
    north = lax.ppermute(halo, "tile", down)
    groups = [
        [(x * CHIPS_Z + z) * CORES + core for z in range(CHIPS_Z)] for x in range(CHIPS_X) for core in range(CORES)
    ]
    own_parts = lax.all_to_all(line_sum, "tile", 0, 0, axis_index_groups=groups, tiled=True)
    tracer_grad = call(
        mixing_kernel,
        shape((own * levels * lines, LANES), F32),
        [VMEM] * 5,
        HBM,
        [
            pltpu.VMEM((levels // SUB, 5, lines // ROWS, SUB, LANES), F32),
            pltpu.VMEM((levels // SUB, 4, lines // ROWS, SUB, LANES), F32),
            pltpu.VMEM((own * levels * lines, LANES), F32),
            pltpu.SemaphoreType.DMA((own,)),
        ],
        pl.CostEstimate(flops=1_000_000, bytes_accessed=2_000_000, transcendentals=0),
    )(col, south, north, depth, params)
    own_parts, tracer_grad = lax.optimization_barrier((own_parts, tracer_grad))
    tile = lax.axis_index("tile")
    place = (tile // (CHIPS_Z * CORES)) * CORES + tile % CORES
    own_parts = own_parts.reshape(CHIPS_Z, CHIPS_X * CORES, own)
    mine = lax.broadcasted_iota(jnp.int32, own_parts.shape, 1) == place
    rate_grad = jnp.sum(jnp.where(mine, own_parts, 0.0), axis=(0, 1))[None]
    tracer_grad = tracer_grad.reshape(own, levels, lines, LANES)
    return (undense(tracer_grad, band_rows), rate_grad)


def solution(mesh):
    return jax.shard_map(
        body,
        mesh=mesh,
        in_specs=(
            P("trc", None, "tile", None),
            P("trc", None, "tile", None),
            P(None, "tile", None),
            P("tile", None),
            P("tile", None),
            P(),
            P(None, "trc"),
            P("trc"),
            P("trc"),
            P("trc"),
        ),
        out_specs=(P("trc", None, "tile", None), P("tile", "trc")),
        check_vma=False,
    )
```

```python
import jax
import jax.numpy as jnp
from jax import lax
from jax.experimental import pallas as pl
from jax.experimental.pallas import tpu as pltpu
from jax.sharding import PartitionSpec as P

SCALE = 256.0
LANES = 128
ROWS = 2
SUB = 8
CHIPS_X, CHIPS_Z, CORES = 4, 8, 2
BF16 = jnp.bfloat16
F32 = jnp.float32
VMEM = pl.BlockSpec(memory_space=pltpu.VMEM)
HBM = pl.BlockSpec(memory_space=pltpu.HBM)
PARAMS = pltpu.CompilerParams(vmem_limit_bytes=40 * 1024 * 1024)


def row(ref, *at):
    *lead, r = at
    blocks = ref.shape[-2] // ROWS
    return ref[(*lead, pl.ds(r, blocks, stride=ROWS), slice(None))]


def wet_at(depth, level):
    return (depth > level).astype(F32)


def weighted_kernel(
    cot_hbm, nutrient_hbm, depth_hbm, region_hbm, rates_hbm, half_hbm, sinking_hbm, mixing_hbm,
    out_ref, params_ref, nutrient_ref, depth_ref, region_ref,
    cot_ref, rates_ref, half_ref, sinking_ref, mixing_ref, held_ref, sems, out_sems,
):
    own, sunlit = held_ref.shape[1], held_ref.shape[0]
    blocks = cot_ref.shape[2] // ROWS
    pairs = [
        (depth_hbm, depth_ref), (region_hbm, region_ref), (rates_hbm, rates_ref), (nutrient_hbm, nutrient_ref),
        (half_hbm, half_ref), (sinking_hbm, sinking_ref), (mixing_hbm, mixing_ref),
    ]
    pairs += [(cot_hbm.at[t, 0:sunlit], cot_ref.at[t]) for t in range(own)]
    copies = [pltpu.make_async_copy(here, there, sems.at[n]) for n, (here, there) in enumerate(pairs)]
    for copy in copies:
        copy.start()
    for copy in copies[: len(pairs) - own]:
        copy.wait()
    depth = [row(depth_ref, r) for r in range(ROWS)]
    region = [row(region_ref, r) for r in range(ROWS)]
    rest = jnp.zeros((1, LANES - rates_ref.shape[1]), F32)
    for t in range(own):
        line = jnp.concatenate([rates_ref[t : t + 1, :], rest], axis=1)
        line = jnp.broadcast_to(line, (blocks, LANES))
        rates = [jnp.take_along_axis(line, region[r], axis=1) for r in range(ROWS)]
        half = half_ref[t]
        for n, ref in enumerate((half_ref, sinking_ref, mixing_ref)):
            params_ref[n * SUB + t : n * SUB + t + 1, :] = jnp.full((1, LANES), ref[t], F32)
        copies[len(pairs) - own + t].wait()
        for k in range(sunlit):
            rows = []
            for r in range(ROWS):
                food = row(nutrient_ref, k, r)
                limiter = food / (food + half)
                grad = row(cot_ref, t, k, r) * wet_at(depth[r], k)
                rows.append(rates[r] * limiter * grad)
            held_ref[k, t] = jnp.concatenate(rows, axis=0).astype(BF16)
        copies.append(pltpu.make_async_copy(held_ref.at[:, t], out_ref.at[:, t], out_sems.at[t]))
        copies[-1].start()
    for copy in copies[-own:]:
        copy.wait()


def province_kernel(cot_ref, uptake_ref, nutrient_ref, depth_ref, region_ref, params_ref, out_ref, hot_ref, term_ref, parts_ref):
    provinces, own = out_ref.shape
    sunlit = nutrient_ref.shape[0]
    lines = depth_ref.shape[0]
    depth = depth_ref[...]
    term_ref[...] = jnp.zeros(term_ref.shape, F32)
    for t in range(own):
        half = jnp.broadcast_to(params_ref[t : t + 1, :], (lines, LANES))
        total = jnp.zeros((lines, LANES), F32)
        for k in range(sunlit):
            food = nutrient_ref[k]
            limiter = food / (food + half)
            grad = cot_ref[t, k] * wet_at(depth, k)
            total = total + limiter * uptake_ref[t, k].astype(F32) * grad
        term_ref[pl.ds(t, lines, stride=8), :] = total
    place = lax.broadcasted_iota(jnp.int32, (provinces, LANES), 0)
    z, x, core = place // (CHIPS_X * CORES), (place // CORES) % CHIPS_X, place % CORES
    ids = (x * CHIPS_Z + z) * CORES + core
    for s in range(lines):
        line = jnp.broadcast_to(region_ref[s : s + 1, :], (provinces, LANES))
        hot_ref[:, s * LANES : (s + 1) * LANES] = (line == ids).astype(F32).astype(BF16)
        term = term_ref[s * 8 : (s + 1) * 8, :]
        high = term.astype(BF16).astype(F32)
        both = jnp.concatenate([high, term - high], axis=0)
        parts_ref[:, s * LANES : (s + 1) * LANES] = both.astype(BF16)
    sums = lax.dot_general(hot_ref[...], parts_ref[...], (((1,), (1,)), ((), ())), preferred_element_type=F32)
    scale = 1.0 / (sunlit * lines * LANES)
    out_ref[...] = (sums[:, 0:own] + sums[:, SUB : SUB + own]) * scale


def feed_kernel(matrix_ref, weighted_ref, out_ref, wide_ref, fed_ref):
    tracers, lines = weighted_ref.shape[0], weighted_ref.shape[1]
    matrix = matrix_ref[...].astype(F32).T.astype(BF16)
    for t in range(tracers):
        wide_ref[t * lines : (t + 1) * lines, :] = weighted_ref[t].astype(F32)
    for s in range(0, lines, 2):
        cells = [wide_ref[pl.ds(s + i, tracers, stride=lines), :].astype(BF16) for i in range(2)]
        fed = jnp.dot(matrix, jnp.concatenate(cells, axis=1), preferred_element_type=F32) * SCALE
        for i in range(2):
            fed_ref[pl.ds(s + i, tracers, stride=lines), :] = fed[:, i * LANES : (i + 1) * LANES]
    for t in range(tracers):
        out_ref[t] = fed_ref[t * lines : (t + 1) * lines, :]


def column_kernel(cot_ref, fed_ref, depth_ref, params_ref, col_ref, halo_ref):
    lines = depth_ref.shape[0]
    blocks = lines // ROWS
    own = col_ref.shape[0] // lines
    levels = col_ref.shape[1]
    blocks_of = [depth_ref[b * ROWS + r : b * ROWS + r + 1, :] for r in range(ROWS) for b in range(blocks)]
    halo_ref[own * lines] = jnp.concatenate(blocks_of, axis=0).astype(F32).astype(BF16)
    ids = lax.broadcasted_iota(jnp.int32, (SUB, LANES), 0)
    bottom = ids == SUB - 1
    for n in range(lines):
        r, b = n // blocks, n % blocks
        depth = jnp.broadcast_to(blocks_of[n], (SUB, LANES))
        top_wet, low_wet = (depth > ids).astype(F32), (depth > ids + SUB).astype(F32)
        top_next = (depth > ids + 1).astype(F32)
        low_next = jnp.where(bottom, 0.0, (depth > ids + SUB + 1).astype(F32))

        for t in range(own):
            base = (t * levels) * lines + b * ROWS + r
            top = cot_ref[pl.ds(base, SUB, stride=lines), :] * top_wet
            low = cot_ref[pl.ds(base + SUB * lines, SUB, stride=lines), :] * low_wet
            fed = fed_ref[pl.ds(t * lines + n, SUB, stride=own * lines), :] * (1.0 / SCALE)
            top = top + top_wet * fed
            low_up = pltpu.roll(low, SUB - 1, 0)
            top_up = jnp.where(bottom, low_up, pltpu.roll(top, SUB - 1, 0))
            sink = params_ref[SUB + t : SUB + t + 1, :]
            col_top = top + sink * top_next * (top_up - top)
            col_low = low + sink * low_next * (low_up - low)
            both = jnp.concatenate([col_top, col_low], axis=0)
            col_ref[t * lines + n] = both
            halo_ref[t * lines + n] = both.astype(BF16)


def mixing_kernel(col_ref, south_ref, north_ref, depth_ref, params_ref, out_hbm, edges_y_ref, edges_x_ref, out_ref, sems):
    lines = depth_ref.shape[0]
    own = col_ref.shape[0] // lines
    blocks = lines // ROWS
    levels = col_ref.shape[1]
    flip = lax.axis_index("tile") & 1
    order = [r ^ flip for r in range(ROWS)]
    halves = levels // SUB
    ids = lax.broadcasted_iota(jnp.int32, (SUB, LANES), 0)
    lane_ids = lax.broadcasted_iota(jnp.int32, (SUB, LANES), 1)
    last_lane, first_lane = lane_ids == LANES - 1, lane_ids == 0

    def east(v):
        turned = [pltpu.roll(x, LANES - 1, 1) for x in v]
        return [jnp.where(last_lane, turned[(b + 1) % blocks], turned[b]) for b in range(blocks)]

    def west(v):
        turned = [pltpu.roll(x, 1, 1) for x in v]
        return [jnp.where(first_lane, turned[(b - 1) % blocks], turned[b]) for b in range(blocks)]

    def own_depth(n):
        r, b = n // blocks, n % blocks
        return jnp.broadcast_to(depth_ref[pl.ds(b * ROWS + order[r], 1), :], (SUB, LANES)).astype(F32)

    def field(which, at, h):
        ref = (south_ref, col_ref, north_ref)[at // ROWS]
        return [ref[which * lines + order[at % ROWS] * blocks + b, h * SUB : (h + 1) * SUB, :].astype(F32) for b in range(blocks)]

    far = [ref[own * lines].astype(F32) for ref in (south_ref, north_ref)]
    far = [jnp.where(flip == 1, jnp.concatenate([x[blocks:], x[:blocks]], axis=0), x) for x in far]
    for h in range(halves):
        at = (ids + h * SUB).astype(F32)
        wet = []
        for i in range(3 * ROWS):
            if i // ROWS == 1:
                depths = [own_depth((i % ROWS) * blocks + b) for b in range(blocks)]
            else:
                band, first = far[i // (2 * ROWS)], (i % ROWS) * blocks
                depths = [jnp.broadcast_to(band[first + b : first + b + 1], (SUB, LANES)) for b in range(blocks)]
            wet.append([(d > at).astype(F32) for d in depths])
        for i in range(3 * ROWS - 1):
            for b in range(blocks):
                edges_y_ref[h, i, b] = wet[i][b] * wet[i + 1][b]
        for i in range(1, 3 * ROWS - 1):
            ahead = east(wet[i])
            for b in range(blocks):
                edges_x_ref[h, i - 1, b] = wet[i][b] * ahead[b]

    def laplacian(rows, h, lo, hi):
        flux = [[edges_y_ref[h, i, b] * (rows[i + 1][b] - rows[i][b]) for b in range(blocks)] for i in range(lo - 1, hi)]
        out = []
        for n, i in enumerate(range(lo, hi)):
            ahead = east(rows[i])
            zonal = [edges_x_ref[h, i - 1, b] * (ahead[b] - rows[i][b]) for b in range(blocks)]
            behind = west(zonal)
            out.append([(flux[n + 1][b] - flux[n][b]) + (zonal[b] - behind[b]) for b in range(blocks)])
        return out

    def copy_out(t):
        part = pl.ds(t * levels * lines, levels * lines)
        return pltpu.make_async_copy(out_ref.at[part], out_hbm.at[part], sems.at[t])

    @pl.loop(0, own)
    def _(t):
        mixing = jnp.broadcast_to(params_ref[pl.ds(2 * SUB + t, 1), :], (SUB, LANES))
        for h in range(halves):
            rows = [field(t, i, h) for i in range(3 * ROWS)]
            once = laplacian(rows, h, 1, 5)
            twice = laplacian([None] + once, h, 2, 4)
            for r in range(ROWS):
                for b in range(blocks):
                    value = rows[ROWS + r][b] - mixing * twice[r][b]
                    out_ref[pl.ds((t * levels + h * SUB) * lines + b * ROWS + order[r], SUB, stride=lines), :] = value
        copy_out(t).start()

    for t in range(own):
        copy_out(t).wait()


def dense(band):
    *lead, rows, zonal = band.shape
    cut = band.reshape(*lead, rows, zonal // LANES, LANES)
    return jnp.swapaxes(cut, -3, -2).reshape(*lead, rows * zonal // LANES, LANES)


def undense(lines, rows):
    *lead, count, _ = lines.shape
    cut = lines.reshape(*lead, count // rows, rows, LANES)
    return jnp.swapaxes(cut, -3, -2).reshape(*lead, rows, count * LANES // rows)


def call(kernel, shapes, ins, outs, scratch=(), cost=None):
    return pl.pallas_call(
        kernel,
        out_shape=shapes,
        in_specs=ins,
        out_specs=outs,
        scratch_shapes=scratch,
        cost_estimate=cost,
        compiler_params=PARAMS,
    )


def body(
    cotangent,
    uptake_rate,
    nutrient,
    depth_levels,
    region_ids,
    uptake_matrix,
    province_rates,
    half_saturation,
    biharmonic,
    sinking,
):
    own, levels, band_rows, zonal = cotangent.shape
    sunlit = uptake_rate.shape[1]
    columns = band_rows * zonal
    lines = columns // LANES
    provinces = province_rates.shape[0]
    tracers = uptake_matrix.shape[0]
    tiles = lax.axis_size("tile")
    within = [(i, i ^ 1) for i in range(tiles)]
    across = [(i, ((i + 1) ^ 1) - 1) for i in range(1, tiles - 1)]
    shape = jax.ShapeDtypeStruct
    cot, uptake, nutrient = dense(cotangent), dense(uptake_rate), dense(nutrient)
    depth, region = dense(depth_levels), dense(region_ids)

    inputs = (cot, nutrient, depth, region, province_rates.T, half_saturation, sinking, biharmonic)
    weighted, params, nutrient, depth, region = call(
        weighted_kernel,
        (
            shape((sunlit, own, lines, LANES), BF16),
            shape((3 * SUB, LANES), F32),
            shape(nutrient.shape, F32),
            shape(depth.shape, jnp.int32),
            shape(region.shape, jnp.int32),
        ),
        [HBM] * 8,
        (HBM,) + (VMEM,) * 4,
        [
            pltpu.VMEM((own, sunlit, lines, LANES), F32),
            pltpu.VMEM((own, provinces), F32),
            pltpu.SMEM((own,), F32),
            pltpu.SMEM((own,), F32),
            pltpu.SMEM((own,), F32),
            pltpu.VMEM((sunlit, own, lines, LANES), BF16),
            pltpu.SemaphoreType.DMA((own + 7,)),
            pltpu.SemaphoreType.DMA((own,)),
        ],
        None,
    )(*(pltpu.with_memory_space_constraint(a, pltpu.HBM) for a in inputs))
    all_tracers = lax.all_to_all(weighted, "trc", 0, 0, tiled=True).reshape(tracers, lines, LANES)
    province_part = call(
        province_kernel,
        shape((provinces, own), F32),
        [VMEM] * 6,
        VMEM,
        [
            pltpu.VMEM((provinces, columns), BF16),
            pltpu.VMEM((lines * SUB, LANES), F32),
            pltpu.VMEM((2 * SUB, columns), BF16),
        ],
    )(cot, uptake, nutrient, depth, region, params)
    def exchanged(part, step):
        return part + lax.ppermute(part, "tile", [(i, i ^ step) for i in range(tiles)])

    chip_sum = exchanged(province_part, 1)
    half_sum = exchanged(chip_sum, CHIPS_Z * CORES)
    all_tracers, _ = lax.optimization_barrier((all_tracers, half_sum))
    line_sum = exchanged(half_sum, 2 * CHIPS_Z * CORES)
    fed = call(
        feed_kernel,
        shape((tracers, lines, LANES), F32),
        [VMEM, VMEM],
        VMEM,
        [pltpu.VMEM((tracers * lines, LANES), F32), pltpu.VMEM((tracers * lines, LANES), F32)],
    )(uptake_matrix, all_tracers)
    fed = fed.astype(jnp.float16).reshape(sunlit, own, lines, LANES)
    fed = lax.all_to_all(fed, "trc", 0, 0, tiled=True)
    fed, _ = lax.optimization_barrier((fed, line_sum))
    fed = fed.astype(F32)
    col, halo = call(
        column_kernel,
        (shape((own * lines, levels, LANES), F32), shape((own * lines + 1, levels, LANES), BF16)),
        [VMEM] * 4,
        (VMEM, VMEM),
    )(cot.reshape(-1, LANES), fed.reshape(-1, LANES), depth, params)
    south = lax.ppermute(halo, "tile", across)
    north = lax.ppermute(halo, "tile", within)
    groups = [
        [(x * CHIPS_Z + z) * CORES + core for z in range(CHIPS_Z)] for x in range(CHIPS_X) for core in range(CORES)
    ]
    own_parts = lax.all_to_all(line_sum, "tile", 0, 0, axis_index_groups=groups, tiled=True)
    tracer_grad = call(
        mixing_kernel,
        shape((own * levels * lines, LANES), F32),
        [VMEM] * 5,
        HBM,
        [
            pltpu.VMEM((levels // SUB, 5, lines // ROWS, SUB, LANES), F32),
            pltpu.VMEM((levels // SUB, 4, lines // ROWS, SUB, LANES), F32),
            pltpu.VMEM((own * levels * lines, LANES), F32),
            pltpu.SemaphoreType.DMA((own,)),
        ],
        pl.CostEstimate(flops=1_000_000, bytes_accessed=2_000_000, transcendentals=0),
    )(col, south, north, depth, params)
    own_parts, tracer_grad = lax.optimization_barrier((own_parts, tracer_grad))
    tile = lax.axis_index("tile")
    place = (tile // (CHIPS_Z * CORES)) * CORES + tile % CORES
    own_parts = own_parts.reshape(CHIPS_Z, CHIPS_X * CORES, own)
    mine = lax.broadcasted_iota(jnp.int32, own_parts.shape, 1) == place
    rate_grad = jnp.sum(jnp.where(mine, own_parts, 0.0), axis=(0, 1))[None]
    tracer_grad = tracer_grad.reshape(own, levels, lines, LANES)
    return (undense(tracer_grad, band_rows), rate_grad)


def solution(mesh):
    return jax.shard_map(
        body,
        mesh=mesh,
        in_specs=(
            P("trc", None, "tile", None),
            P("trc", None, "tile", None),
            P(None, "tile", None),
            P("tile", None),
            P("tile", None),
            P(),
            P(None, "trc"),
            P("trc"),
            P("trc"),
            P("trc"),
        ),
        out_specs=(P("trc", None, "tile", None), P("tile", "trc")),
        check_vma=False,
    )
```

```python
import jax
import jax.numpy as jnp
from jax import lax
from jax.experimental import pallas as pl
from jax.experimental.pallas import tpu as pltpu
from jax.sharding import PartitionSpec as P

SCALE = 256.0
LANES = 128
ROWS = 2
SUB = 8
CHIPS_X, CHIPS_Z, CORES = 4, 8, 2
BF16 = jnp.bfloat16
F32 = jnp.float32
VMEM = pl.BlockSpec(memory_space=pltpu.VMEM)
HBM = pl.BlockSpec(memory_space=pltpu.HBM)
PARAMS = pltpu.CompilerParams(vmem_limit_bytes=40 * 1024 * 1024)


def row(ref, *at):
    *lead, r = at
    blocks = ref.shape[-2] // ROWS
    return ref[(*lead, pl.ds(r, blocks, stride=ROWS), slice(None))]


def wet_at(depth, level):
    return (depth > level).astype(F32)


def weighted_kernel(
    cot_hbm, nutrient_hbm, depth_hbm, region_hbm, rates_hbm, half_hbm, sinking_hbm, mixing_hbm,
    out_ref, params_ref, nutrient_ref, depth_ref, region_ref,
    cot_ref, rates_ref, half_ref, sinking_ref, mixing_ref, held_ref, sems, out_sems,
):
    own, sunlit = held_ref.shape[1], held_ref.shape[0]
    blocks = cot_ref.shape[2] // ROWS
    pairs = [
        (depth_hbm, depth_ref), (region_hbm, region_ref), (rates_hbm, rates_ref), (nutrient_hbm, nutrient_ref),
        (half_hbm, half_ref), (sinking_hbm, sinking_ref), (mixing_hbm, mixing_ref),
    ]
    pairs += [(cot_hbm.at[t, 0:sunlit], cot_ref.at[t]) for t in range(own)]
    copies = [pltpu.make_async_copy(here, there, sems.at[n]) for n, (here, there) in enumerate(pairs)]
    for copy in copies:
        copy.start()
    for copy in copies[: len(pairs) - own]:
        copy.wait()
    depth = [row(depth_ref, r) for r in range(ROWS)]
    region = [row(region_ref, r) for r in range(ROWS)]
    rest = jnp.zeros((1, LANES - rates_ref.shape[1]), F32)
    for t in range(own):
        line = jnp.concatenate([rates_ref[t : t + 1, :], rest], axis=1)
        line = jnp.broadcast_to(line, (blocks, LANES))
        rates = [jnp.take_along_axis(line, region[r], axis=1) for r in range(ROWS)]
        half = half_ref[t]
        for n, ref in enumerate((half_ref, sinking_ref, mixing_ref)):
            params_ref[n * SUB + t : n * SUB + t + 1, :] = jnp.full((1, LANES), ref[t], F32)
        copies[len(pairs) - own + t].wait()
        for k in range(sunlit):
            rows = []
            for r in range(ROWS):
                food = row(nutrient_ref, k, r)
                limiter = food / (food + half)
                grad = row(cot_ref, t, k, r) * wet_at(depth[r], k)
                rows.append(rates[r] * limiter * grad)
            held_ref[k, t] = jnp.concatenate(rows, axis=0).astype(BF16)
        copies.append(pltpu.make_async_copy(held_ref.at[:, t], out_ref.at[:, t], out_sems.at[t]))
        copies[-1].start()
    for copy in copies[-own:]:
        copy.wait()


def province_kernel(cot_ref, uptake_ref, nutrient_ref, depth_ref, region_ref, params_ref, out_ref, hot_ref, term_ref, parts_ref):
    provinces, own = out_ref.shape
    sunlit = nutrient_ref.shape[0]
    lines = depth_ref.shape[0]
    depth = depth_ref[...]
    term_ref[...] = jnp.zeros(term_ref.shape, F32)
    for t in range(own):
        half = jnp.broadcast_to(params_ref[t : t + 1, :], (lines, LANES))
        total = jnp.zeros((lines, LANES), F32)
        for k in range(sunlit):
            food = nutrient_ref[k]
            limiter = food / (food + half)
            grad = cot_ref[t, k] * wet_at(depth, k)
            total = total + limiter * uptake_ref[t, k].astype(F32) * grad
        term_ref[pl.ds(t, lines, stride=8), :] = total
    place = lax.broadcasted_iota(jnp.int32, (provinces, LANES), 0)
    z, x, core = CHIPS_Z - 1 - place // (CHIPS_X * CORES), (place // CORES) % CHIPS_X, place % CORES
    ids = (x * CHIPS_Z + z) * CORES + core
    for s in range(lines):
        line = jnp.broadcast_to(region_ref[s : s + 1, :], (provinces, LANES))
        hot_ref[:, s * LANES : (s + 1) * LANES] = (line == ids).astype(F32).astype(BF16)
        term = term_ref[s * 8 : (s + 1) * 8, :]
        high = term.astype(BF16).astype(F32)
        both = jnp.concatenate([high, term - high], axis=0)
        parts_ref[:, s * LANES : (s + 1) * LANES] = both.astype(BF16)
    sums = lax.dot_general(hot_ref[...], parts_ref[...], (((1,), (1,)), ((), ())), preferred_element_type=F32)
    scale = 1.0 / (sunlit * lines * LANES)
    out_ref[...] = (sums[:, 0:own] + sums[:, SUB : SUB + own]) * scale


def feed_kernel(matrix_ref, weighted_ref, out_ref, wide_ref, fed_ref):
    tracers, lines = weighted_ref.shape[0], weighted_ref.shape[1]
    matrix = matrix_ref[...].astype(F32).T.astype(BF16)
    for t in range(tracers):
        wide_ref[t * lines : (t + 1) * lines, :] = weighted_ref[t].astype(F32)
    for s in range(0, lines, 2):
        cells = [wide_ref[pl.ds(s + i, tracers, stride=lines), :].astype(BF16) for i in range(2)]
        fed = jnp.dot(matrix, jnp.concatenate(cells, axis=1), preferred_element_type=F32) * SCALE
        for i in range(2):
            fed_ref[pl.ds(s + i, tracers, stride=lines), :] = fed[:, i * LANES : (i + 1) * LANES]
    for t in range(tracers):
        out_ref[t] = fed_ref[t * lines : (t + 1) * lines, :]


def column_kernel(cot_ref, fed_ref, depth_ref, params_ref, col_ref, halo_ref):
    lines = depth_ref.shape[0]
    blocks = lines // ROWS
    own = col_ref.shape[0] // lines
    levels = col_ref.shape[1]
    blocks_of = [depth_ref[b * ROWS + r : b * ROWS + r + 1, :] for r in range(ROWS) for b in range(blocks)]
    halo_ref[own * lines] = jnp.concatenate(blocks_of, axis=0).astype(F32).astype(BF16)
    ids = lax.broadcasted_iota(jnp.int32, (SUB, LANES), 0)
    bottom = ids == SUB - 1
    for n in range(lines):
        r, b = n // blocks, n % blocks
        depth = jnp.broadcast_to(blocks_of[n], (SUB, LANES))
        top_wet, low_wet = (depth > ids).astype(F32), (depth > ids + SUB).astype(F32)
        top_next = (depth > ids + 1).astype(F32)
        low_next = jnp.where(bottom, 0.0, (depth > ids + SUB + 1).astype(F32))

        for t in range(own):
            base = (t * levels) * lines + b * ROWS + r
            top = cot_ref[pl.ds(base, SUB, stride=lines), :] * top_wet
            low = cot_ref[pl.ds(base + SUB * lines, SUB, stride=lines), :] * low_wet
            fed = fed_ref[pl.ds(t * lines + n, SUB, stride=own * lines), :] * (1.0 / SCALE)
            top = top + top_wet * fed
            low_up = pltpu.roll(low, SUB - 1, 0)
            top_up = jnp.where(bottom, low_up, pltpu.roll(top, SUB - 1, 0))
            sink = params_ref[SUB + t : SUB + t + 1, :]
            col_top = top + sink * top_next * (top_up - top)
            col_low = low + sink * low_next * (low_up - low)
            both = jnp.concatenate([col_top, col_low], axis=0)
            col_ref[t * lines + n] = both
            halo_ref[t * lines + n] = both.astype(BF16)


def mixing_kernel(col_ref, south_ref, north_ref, depth_ref, params_ref, out_hbm, edges_y_ref, edges_x_ref, out_ref, sems):
    lines = depth_ref.shape[0]
    own = col_ref.shape[0] // lines
    blocks = lines // ROWS
    levels = col_ref.shape[1]
    flip = lax.axis_index("tile") & 1
    order = [r ^ flip for r in range(ROWS)]
    halves = levels // SUB
    ids = lax.broadcasted_iota(jnp.int32, (SUB, LANES), 0)
    lane_ids = lax.broadcasted_iota(jnp.int32, (SUB, LANES), 1)
    last_lane, first_lane = lane_ids == LANES - 1, lane_ids == 0

    def east(v):
        turned = [pltpu.roll(x, LANES - 1, 1) for x in v]
        return [jnp.where(last_lane, turned[(b + 1) % blocks], turned[b]) for b in range(blocks)]

    def west(v):
        turned = [pltpu.roll(x, 1, 1) for x in v]
        return [jnp.where(first_lane, turned[(b - 1) % blocks], turned[b]) for b in range(blocks)]

    def own_depth(n):
        r, b = n // blocks, n % blocks
        return jnp.broadcast_to(depth_ref[pl.ds(b * ROWS + order[r], 1), :], (SUB, LANES)).astype(F32)

    def field(which, at, h):
        ref = (south_ref, col_ref, north_ref)[at // ROWS]
        return [ref[which * lines + order[at % ROWS] * blocks + b, h * SUB : (h + 1) * SUB, :].astype(F32) for b in range(blocks)]

    far = [ref[own * lines].astype(F32) for ref in (south_ref, north_ref)]
    far = [jnp.where(flip == 1, jnp.concatenate([x[blocks:], x[:blocks]], axis=0), x) for x in far]
    for h in range(halves):
        at = (ids + h * SUB).astype(F32)
        wet = []
        for i in range(3 * ROWS):
            if i // ROWS == 1:
                depths = [own_depth((i % ROWS) * blocks + b) for b in range(blocks)]
            else:
                band, first = far[i // (2 * ROWS)], (i % ROWS) * blocks
                depths = [jnp.broadcast_to(band[first + b : first + b + 1], (SUB, LANES)) for b in range(blocks)]
            wet.append([(d > at).astype(F32) for d in depths])
        for i in range(3 * ROWS - 1):
            for b in range(blocks):
                edges_y_ref[h, i, b] = wet[i][b] * wet[i + 1][b]
        for i in range(1, 3 * ROWS - 1):
            ahead = east(wet[i])
            for b in range(blocks):
                edges_x_ref[h, i - 1, b] = wet[i][b] * ahead[b]

    def laplacian(rows, h, lo, hi):
        flux = [[edges_y_ref[h, i, b] * (rows[i + 1][b] - rows[i][b]) for b in range(blocks)] for i in range(lo - 1, hi)]
        out = []
        for n, i in enumerate(range(lo, hi)):
            ahead = east(rows[i])
            zonal = [edges_x_ref[h, i - 1, b] * (ahead[b] - rows[i][b]) for b in range(blocks)]
            behind = west(zonal)
            out.append([(flux[n + 1][b] - flux[n][b]) + (zonal[b] - behind[b]) for b in range(blocks)])
        return out

    def copy_out(t):
        part = pl.ds(t * levels * lines, levels * lines)
        return pltpu.make_async_copy(out_ref.at[part], out_hbm.at[part], sems.at[t])

    @pl.loop(0, own)
    def _(t):
        mixing = jnp.broadcast_to(params_ref[pl.ds(2 * SUB + t, 1), :], (SUB, LANES))
        for h in range(halves):
            rows = [field(t, i, h) for i in range(3 * ROWS)]
            once = laplacian(rows, h, 1, 5)
            twice = laplacian([None] + once, h, 2, 4)
            for r in range(ROWS):
                for b in range(blocks):
                    value = rows[ROWS + r][b] - mixing * twice[r][b]
                    out_ref[pl.ds((t * levels + h * SUB) * lines + b * ROWS + order[r], SUB, stride=lines), :] = value
        copy_out(t).start()

    for t in range(own):
        copy_out(t).wait()


def dense(band):
    *lead, rows, zonal = band.shape
    cut = band.reshape(*lead, rows, zonal // LANES, LANES)
    return jnp.swapaxes(cut, -3, -2).reshape(*lead, rows * zonal // LANES, LANES)


def undense(lines, rows):
    *lead, count, _ = lines.shape
    cut = lines.reshape(*lead, count // rows, rows, LANES)
    return jnp.swapaxes(cut, -3, -2).reshape(*lead, rows, count * LANES // rows)


def call(kernel, shapes, ins, outs, scratch=(), cost=None):
    return pl.pallas_call(
        kernel,
        out_shape=shapes,
        in_specs=ins,
        out_specs=outs,
        scratch_shapes=scratch,
        cost_estimate=cost,
        compiler_params=PARAMS,
    )


def body(
    cotangent,
    uptake_rate,
    nutrient,
    depth_levels,
    region_ids,
    uptake_matrix,
    province_rates,
    half_saturation,
    biharmonic,
    sinking,
):
    own, levels, band_rows, zonal = cotangent.shape
    sunlit = uptake_rate.shape[1]
    columns = band_rows * zonal
    lines = columns // LANES
    provinces = province_rates.shape[0]
    tracers = uptake_matrix.shape[0]
    tiles = lax.axis_size("tile")
    within = [(i, i ^ 1) for i in range(tiles)]
    across = [(i, ((i + 1) ^ 1) - 1) for i in range(1, tiles - 1)]
    shape = jax.ShapeDtypeStruct
    cot, uptake, nutrient = dense(cotangent), dense(uptake_rate), dense(nutrient)
    depth, region = dense(depth_levels), dense(region_ids)

    inputs = (cot, nutrient, depth, region, province_rates.T, half_saturation, sinking, biharmonic)
    weighted, params, nutrient, depth, region = call(
        weighted_kernel,
        (
            shape((sunlit, own, lines, LANES), BF16),
            shape((3 * SUB, LANES), F32),
            shape(nutrient.shape, F32),
            shape(depth.shape, jnp.int32),
            shape(region.shape, jnp.int32),
        ),
        [HBM] * 8,
        (HBM,) + (VMEM,) * 4,
        [
            pltpu.VMEM((own, sunlit, lines, LANES), F32),
            pltpu.VMEM((own, provinces), F32),
            pltpu.SMEM((own,), F32),
            pltpu.SMEM((own,), F32),
            pltpu.SMEM((own,), F32),
            pltpu.VMEM((sunlit, own, lines, LANES), BF16),
            pltpu.SemaphoreType.DMA((own + 7,)),
            pltpu.SemaphoreType.DMA((own,)),
        ],
        None,
    )(*(pltpu.with_memory_space_constraint(a, pltpu.HBM) for a in inputs))
    all_tracers = lax.all_to_all(weighted, "trc", 0, 0, tiled=True).reshape(tracers, lines, LANES)
    province_part = call(
        province_kernel,
        shape((provinces, own), F32),
        [VMEM] * 6,
        VMEM,
        [
            pltpu.VMEM((provinces, columns), BF16),
            pltpu.VMEM((lines * SUB, LANES), F32),
            pltpu.VMEM((2 * SUB, columns), BF16),
        ],
    )(cot, uptake, nutrient, depth, region, params)
    def exchanged(part, step):
        return part + lax.ppermute(part, "tile", [(i, i ^ step) for i in range(tiles)])

    chip_sum = exchanged(province_part, 1)
    other_half = lax.ppermute(chip_sum, "tile", [(i, i ^ (CHIPS_Z * CORES)) for i in range(tiles)])
    all_tracers, _ = lax.optimization_barrier((all_tracers, chip_sum))
    fed = call(
        feed_kernel,
        shape((tracers, lines, LANES), F32),
        [VMEM, VMEM],
        VMEM,
        [pltpu.VMEM((tracers * lines, LANES), F32), pltpu.VMEM((tracers * lines, LANES), F32)],
    )(uptake_matrix, all_tracers)
    fed = fed.astype(jnp.float16).reshape(sunlit, own, lines, LANES)
    fed, chip_sum = lax.optimization_barrier((fed, chip_sum))
    half_sum = chip_sum + other_half
    fed, half_sum = lax.optimization_barrier((fed, half_sum))
    line_sum = exchanged(half_sum, 2 * CHIPS_Z * CORES)
    fed = lax.all_to_all(fed, "trc", 0, 0, tiled=True)
    fed, _ = lax.optimization_barrier((fed, line_sum))
    fed = fed.astype(F32)
    col, halo = call(
        column_kernel,
        (shape((own * lines, levels, LANES), F32), shape((own * lines + 1, levels, LANES), BF16)),
        [VMEM] * 4,
        (VMEM, VMEM),
    )(cot.reshape(-1, LANES), fed.reshape(-1, LANES), depth, params)
    south = lax.ppermute(halo, "tile", across)
    north = lax.ppermute(halo, "tile", within)
    groups = [
        [(x * CHIPS_Z + z) * CORES + core for z in reversed(range(CHIPS_Z))] for x in range(CHIPS_X) for core in range(CORES)
    ]
    own_parts = lax.all_to_all(line_sum, "tile", 0, 0, axis_index_groups=groups, tiled=True)
    tracer_grad = call(
        mixing_kernel,
        shape((own * levels * lines, LANES), F32),
        [VMEM] * 5,
        HBM,
        [
            pltpu.VMEM((levels // SUB, 5, lines // ROWS, SUB, LANES), F32),
            pltpu.VMEM((levels // SUB, 4, lines // ROWS, SUB, LANES), F32),
            pltpu.VMEM((own * levels * lines, LANES), F32),
            pltpu.SemaphoreType.DMA((own,)),
        ],
        pl.CostEstimate(flops=1_000_000, bytes_accessed=2_000_000, transcendentals=0),
    )(col, south, north, depth, params)
    own_parts, tracer_grad = lax.optimization_barrier((own_parts, tracer_grad))
    tile = lax.axis_index("tile")
    place = (tile // (CHIPS_Z * CORES)) * CORES + tile % CORES
    own_parts = own_parts.reshape(CHIPS_Z, CHIPS_X * CORES, own)
    mine = lax.broadcasted_iota(jnp.int32, own_parts.shape, 1) == place
    rate_grad = jnp.sum(jnp.where(mine, own_parts, 0.0), axis=(0, 1))[None]
    tracer_grad = tracer_grad.reshape(own, levels, lines, LANES)
    return (undense(tracer_grad, band_rows), rate_grad)


def solution(mesh):
    return jax.shard_map(
        body,
        mesh=mesh,
        in_specs=(
            P("trc", None, "tile", None),
            P("trc", None, "tile", None),
            P(None, "tile", None),
            P("tile", None),
            P("tile", None),
            P(),
            P(None, "trc"),
            P("trc"),
            P("trc"),
            P("trc"),
        ),
        out_specs=(P("trc", None, "tile", None), P("tile", "trc")),
        check_vma=False,
    )
```

```python
import jax
import jax.numpy as jnp
from jax import lax
from jax.experimental import pallas as pl
from jax.experimental.pallas import tpu as pltpu
from jax.sharding import PartitionSpec as P

SCALE = 256.0
LANES = 128
ROWS = 2
SUB = 8
CHIPS_X, CHIPS_Z, CORES = 4, 8, 2
BF16 = jnp.bfloat16
F32 = jnp.float32
VMEM = pl.BlockSpec(memory_space=pltpu.VMEM)
HBM = pl.BlockSpec(memory_space=pltpu.HBM)
PARAMS = pltpu.CompilerParams(vmem_limit_bytes=40 * 1024 * 1024)


def row(ref, *at):
    *lead, r = at
    blocks = ref.shape[-2] // ROWS
    return ref[(*lead, pl.ds(r, blocks, stride=ROWS), slice(None))]


def wet_at(depth, level):
    return (depth > level).astype(F32)


def weighted_kernel(
    cot_hbm, nutrient_hbm, depth_hbm, region_hbm, rates_hbm, half_hbm, sinking_hbm, mixing_hbm,
    out_ref, params_ref, nutrient_ref, depth_ref, region_ref,
    cot_ref, rates_ref, half_ref, sinking_ref, mixing_ref, held_ref, sems, out_sems,
):
    own, sunlit = held_ref.shape[1], held_ref.shape[0]
    blocks = cot_ref.shape[2] // ROWS
    pairs = [
        (depth_hbm, depth_ref), (region_hbm, region_ref), (rates_hbm, rates_ref), (nutrient_hbm, nutrient_ref),
        (half_hbm, half_ref), (sinking_hbm, sinking_ref), (mixing_hbm, mixing_ref),
    ]
    pairs += [(cot_hbm.at[t, 0:sunlit], cot_ref.at[t]) for t in range(own)]
    copies = [pltpu.make_async_copy(here, there, sems.at[n]) for n, (here, there) in enumerate(pairs)]
    for copy in copies:
        copy.start()
    for copy in copies[: len(pairs) - own]:
        copy.wait()
    depth = [row(depth_ref, r) for r in range(ROWS)]
    region = [row(region_ref, r) for r in range(ROWS)]
    rest = jnp.zeros((1, LANES - rates_ref.shape[1]), F32)
    for t in range(own):
        line = jnp.concatenate([rates_ref[t : t + 1, :], rest], axis=1)
        line = jnp.broadcast_to(line, (blocks, LANES))
        rates = [jnp.take_along_axis(line, region[r], axis=1) for r in range(ROWS)]
        half = half_ref[t]
        for n, ref in enumerate((half_ref, sinking_ref, mixing_ref)):
            params_ref[n * SUB + t : n * SUB + t + 1, :] = jnp.full((1, LANES), ref[t], F32)
        copies[len(pairs) - own + t].wait()
        for k in range(sunlit):
            rows = []
            for r in range(ROWS):
                food = row(nutrient_ref, k, r)
                limiter = food / (food + half)
                grad = row(cot_ref, t, k, r) * wet_at(depth[r], k)
                rows.append(rates[r] * limiter * grad)
            held_ref[k, t] = jnp.concatenate(rows, axis=0).astype(BF16)
        copies.append(pltpu.make_async_copy(held_ref.at[:, t], out_ref.at[:, t], out_sems.at[t]))
        copies[-1].start()
    for copy in copies[-own:]:
        copy.wait()


def province_kernel(cot_ref, uptake_ref, nutrient_ref, depth_ref, region_ref, params_ref, matrix_ref, out_ref, turned_ref, hot_ref, term_ref, parts_ref):
    provinces, own = out_ref.shape

    def reversed_blocks(m):
        return jnp.concatenate([m[i : i + own] for i in range(m.shape[0] - own, -1, -own)], axis=0)

    turned_ref[...] = reversed_blocks(reversed_blocks(matrix_ref[...].astype(F32)).T).astype(BF16)
    sunlit = nutrient_ref.shape[0]
    lines = depth_ref.shape[0]
    depth = depth_ref[...]
    term_ref[...] = jnp.zeros(term_ref.shape, F32)
    for t in range(own):
        half = jnp.broadcast_to(params_ref[t : t + 1, :], (lines, LANES))
        total = jnp.zeros((lines, LANES), F32)
        for k in range(sunlit):
            food = nutrient_ref[k]
            limiter = food / (food + half)
            grad = cot_ref[t, k] * wet_at(depth, k)
            total = total + limiter * uptake_ref[t, k].astype(F32) * grad
        term_ref[pl.ds(t, lines, stride=8), :] = total
    place = lax.broadcasted_iota(jnp.int32, (provinces, LANES), 0)
    z, x, core = CHIPS_Z - 1 - place // (CHIPS_X * CORES), (place // CORES) % CHIPS_X, place % CORES
    ids = (x * CHIPS_Z + z) * CORES + core
    for s in range(lines):
        line = jnp.broadcast_to(region_ref[s : s + 1, :], (provinces, LANES))
        hot_ref[:, s * LANES : (s + 1) * LANES] = (line == ids).astype(F32).astype(BF16)
        term = term_ref[s * 8 : (s + 1) * 8, :]
        high = term.astype(BF16).astype(F32)
        both = jnp.concatenate([high, term - high], axis=0)
        parts_ref[:, s * LANES : (s + 1) * LANES] = both.astype(BF16)
    sums = lax.dot_general(hot_ref[...], parts_ref[...], (((1,), (1,)), ((), ())), preferred_element_type=F32)
    scale = 1.0 / (sunlit * lines * LANES)
    out_ref[...] = (sums[:, 0:own] + sums[:, SUB : SUB + own]) * scale


def feed_kernel(matrix_ref, weighted_ref, out_ref, wide_ref, fed_ref):
    tracers, lines = weighted_ref.shape[0], weighted_ref.shape[1]
    matrix = matrix_ref[...]
    for t in range(tracers):
        wide_ref[t * lines : (t + 1) * lines, :] = weighted_ref[t].astype(F32)
    for s in range(0, lines, 2):
        cells = [wide_ref[pl.ds(s + i, tracers, stride=lines), :].astype(BF16) for i in range(2)]
        fed = jnp.dot(matrix, jnp.concatenate(cells, axis=1), preferred_element_type=F32) * SCALE
        for i in range(2):
            fed_ref[pl.ds(s + i, tracers, stride=lines), :] = fed[:, i * LANES : (i + 1) * LANES]
    for t in range(tracers):
        out_ref[t] = fed_ref[t * lines : (t + 1) * lines, :]


def column_kernel(cot_ref, fed_ref, depth_ref, params_ref, col_ref, halo_ref):
    lines = depth_ref.shape[0]
    blocks = lines // ROWS
    own = col_ref.shape[0] // lines
    levels = col_ref.shape[1]
    blocks_of = [depth_ref[b * ROWS + r : b * ROWS + r + 1, :] for r in range(ROWS) for b in range(blocks)]
    halo_ref[own * lines] = jnp.concatenate(blocks_of, axis=0).astype(F32).astype(BF16)
    ids = lax.broadcasted_iota(jnp.int32, (SUB, LANES), 0)
    bottom = ids == SUB - 1
    for n in range(lines):
        r, b = n // blocks, n % blocks
        depth = jnp.broadcast_to(blocks_of[n], (SUB, LANES))
        top_wet, low_wet = (depth > ids).astype(F32), (depth > ids + SUB).astype(F32)
        top_next = (depth > ids + 1).astype(F32)
        low_next = jnp.where(bottom, 0.0, (depth > ids + SUB + 1).astype(F32))

        for t in range(own):
            base = (t * levels) * lines + b * ROWS + r
            top = cot_ref[pl.ds(base, SUB, stride=lines), :] * top_wet
            low = cot_ref[pl.ds(base + SUB * lines, SUB, stride=lines), :] * low_wet
            fed = fed_ref[pl.ds(t * lines + n, SUB, stride=own * lines), :] * (1.0 / SCALE)
            top = top + top_wet * fed
            low_up = pltpu.roll(low, SUB - 1, 0)
            top_up = jnp.where(bottom, low_up, pltpu.roll(top, SUB - 1, 0))
            sink = params_ref[SUB + t : SUB + t + 1, :]
            col_top = top + sink * top_next * (top_up - top)
            col_low = low + sink * low_next * (low_up - low)
            both = jnp.concatenate([col_top, col_low], axis=0)
            col_ref[t * lines + n] = both
            halo_ref[t * lines + n] = both.astype(BF16)


def mixing_kernel(col_ref, south_ref, north_ref, depth_ref, params_ref, out_hbm, edges_y_ref, edges_x_ref, out_ref, sems):
    lines = depth_ref.shape[0]
    own = col_ref.shape[0] // lines
    blocks = lines // ROWS
    levels = col_ref.shape[1]
    flip = lax.axis_index("tile") & 1
    order = [r ^ flip for r in range(ROWS)]
    halves = levels // SUB
    ids = lax.broadcasted_iota(jnp.int32, (SUB, LANES), 0)
    lane_ids = lax.broadcasted_iota(jnp.int32, (SUB, LANES), 1)
    last_lane, first_lane = lane_ids == LANES - 1, lane_ids == 0

    def east(v):
        turned = [pltpu.roll(x, LANES - 1, 1) for x in v]
        return [jnp.where(last_lane, turned[(b + 1) % blocks], turned[b]) for b in range(blocks)]

    def west(v):
        turned = [pltpu.roll(x, 1, 1) for x in v]
        return [jnp.where(first_lane, turned[(b - 1) % blocks], turned[b]) for b in range(blocks)]

    def own_depth(n):
        r, b = n // blocks, n % blocks
        return jnp.broadcast_to(depth_ref[pl.ds(b * ROWS + order[r], 1), :], (SUB, LANES)).astype(F32)

    def field(which, at, h):
        ref = (south_ref, col_ref, north_ref)[at // ROWS]
        return [ref[which * lines + order[at % ROWS] * blocks + b, h * SUB : (h + 1) * SUB, :].astype(F32) for b in range(blocks)]

    far = [ref[own * lines].astype(F32) for ref in (south_ref, north_ref)]
    far = [jnp.where(flip == 1, jnp.concatenate([x[blocks:], x[:blocks]], axis=0), x) for x in far]
    for h in range(halves):
        at = (ids + h * SUB).astype(F32)
        wet = []
        for i in range(3 * ROWS):
            if i // ROWS == 1:
                depths = [own_depth((i % ROWS) * blocks + b) for b in range(blocks)]
            else:
                band, first = far[i // (2 * ROWS)], (i % ROWS) * blocks
                depths = [jnp.broadcast_to(band[first + b : first + b + 1], (SUB, LANES)) for b in range(blocks)]
            wet.append([(d > at).astype(F32) for d in depths])
        for i in range(3 * ROWS - 1):
            for b in range(blocks):
                edges_y_ref[h, i, b] = wet[i][b] * wet[i + 1][b]
        for i in range(1, 3 * ROWS - 1):
            ahead = east(wet[i])
            for b in range(blocks):
                edges_x_ref[h, i - 1, b] = wet[i][b] * ahead[b]

    def laplacian(rows, h, lo, hi):
        flux = [[edges_y_ref[h, i, b] * (rows[i + 1][b] - rows[i][b]) for b in range(blocks)] for i in range(lo - 1, hi)]
        out = []
        for n, i in enumerate(range(lo, hi)):
            ahead = east(rows[i])
            zonal = [edges_x_ref[h, i - 1, b] * (ahead[b] - rows[i][b]) for b in range(blocks)]
            behind = west(zonal)
            out.append([(flux[n + 1][b] - flux[n][b]) + (zonal[b] - behind[b]) for b in range(blocks)])
        return out

    def copy_out(t):
        part = pl.ds(t * levels * lines, levels * lines)
        return pltpu.make_async_copy(out_ref.at[part], out_hbm.at[part], sems.at[t])

    @pl.loop(0, own)
    def _(t):
        mixing = jnp.broadcast_to(params_ref[pl.ds(2 * SUB + t, 1), :], (SUB, LANES))
        for h in range(halves):
            rows = [field(t, i, h) for i in range(3 * ROWS)]
            once = laplacian(rows, h, 1, 5)
            twice = laplacian([None] + once, h, 2, 4)
            for r in range(ROWS):
                for b in range(blocks):
                    value = rows[ROWS + r][b] - mixing * twice[r][b]
                    out_ref[pl.ds((t * levels + h * SUB) * lines + b * ROWS + order[r], SUB, stride=lines), :] = value
        copy_out(t).start()

    for t in range(own):
        copy_out(t).wait()


def dense(band):
    *lead, rows, zonal = band.shape
    cut = band.reshape(*lead, rows, zonal // LANES, LANES)
    return jnp.swapaxes(cut, -3, -2).reshape(*lead, rows * zonal // LANES, LANES)


def undense(lines, rows):
    *lead, count, _ = lines.shape
    cut = lines.reshape(*lead, count // rows, rows, LANES)
    return jnp.swapaxes(cut, -3, -2).reshape(*lead, rows, count * LANES // rows)


def call(kernel, shapes, ins, outs, scratch=(), cost=None):
    return pl.pallas_call(
        kernel,
        out_shape=shapes,
        in_specs=ins,
        out_specs=outs,
        scratch_shapes=scratch,
        cost_estimate=cost,
        compiler_params=PARAMS,
    )


def body(
    cotangent,
    uptake_rate,
    nutrient,
    depth_levels,
    region_ids,
    uptake_matrix,
    province_rates,
    half_saturation,
    biharmonic,
    sinking,
):
    own, levels, band_rows, zonal = cotangent.shape
    sunlit = uptake_rate.shape[1]
    columns = band_rows * zonal
    lines = columns // LANES
    provinces = province_rates.shape[0]
    tracers = uptake_matrix.shape[0]
    tiles = lax.axis_size("tile")
    within = [(i, i ^ 1) for i in range(tiles)]
    across = [(i, ((i + 1) ^ 1) - 1) for i in range(1, tiles - 1)]
    shape = jax.ShapeDtypeStruct
    cot, uptake, nutrient = dense(cotangent), dense(uptake_rate), dense(nutrient)
    depth, region = dense(depth_levels), dense(region_ids)

    inputs = (cot, nutrient, depth, region, province_rates.T, half_saturation, sinking, biharmonic)
    weighted, params, nutrient, depth, region = call(
        weighted_kernel,
        (
            shape((sunlit, own, lines, LANES), BF16),
            shape((3 * SUB, LANES), F32),
            shape(nutrient.shape, F32),
            shape(depth.shape, jnp.int32),
            shape(region.shape, jnp.int32),
        ),
        [HBM] * 8,
        (HBM,) + (VMEM,) * 4,
        [
            pltpu.VMEM((own, sunlit, lines, LANES), F32),
            pltpu.VMEM((own, provinces), F32),
            pltpu.SMEM((own,), F32),
            pltpu.SMEM((own,), F32),
            pltpu.SMEM((own,), F32),
            pltpu.VMEM((sunlit, own, lines, LANES), BF16),
            pltpu.SemaphoreType.DMA((own + 7,)),
            pltpu.SemaphoreType.DMA((own,)),
        ],
        None,
    )(*(pltpu.with_memory_space_constraint(a, pltpu.HBM) for a in inputs))
    order_y = [list(reversed(range(lax.axis_size("trc"))))]
    all_tracers = lax.all_to_all(weighted, "trc", 0, 0, axis_index_groups=order_y, tiled=True).reshape(tracers, lines, LANES)
    province_part, turned = call(
        province_kernel,
        (shape((provinces, own), F32), shape(uptake_matrix.shape, BF16)),
        [VMEM] * 7,
        (VMEM,) * 2,
        [
            pltpu.VMEM((provinces, columns), BF16),
            pltpu.VMEM((lines * SUB, LANES), F32),
            pltpu.VMEM((2 * SUB, columns), BF16),
        ],
    )(cot, uptake, nutrient, depth, region, params, uptake_matrix)
    def exchanged(part, step):
        return part + lax.ppermute(part, "tile", [(i, i ^ step) for i in range(tiles)])

    chip_sum = exchanged(province_part, 1)
    other_half = lax.ppermute(chip_sum, "tile", [(i, i ^ (CHIPS_Z * CORES)) for i in range(tiles)])
    all_tracers, _ = lax.optimization_barrier((all_tracers, chip_sum))
    fed = call(
        feed_kernel,
        shape((tracers, lines, LANES), F32),
        [VMEM, VMEM],
        VMEM,
        [pltpu.VMEM((tracers * lines, LANES), F32), pltpu.VMEM((tracers * lines, LANES), F32)],
    )(turned, all_tracers)
    fed = fed.astype(jnp.float16).reshape(sunlit, own, lines, LANES)
    fed, chip_sum = lax.optimization_barrier((fed, chip_sum))
    half_sum = chip_sum + other_half
    fed, half_sum = lax.optimization_barrier((fed, half_sum))
    line_sum = exchanged(half_sum, 2 * CHIPS_Z * CORES)
    fed = lax.all_to_all(fed, "trc", 0, 0, axis_index_groups=order_y, tiled=True)
    fed, _ = lax.optimization_barrier((fed, line_sum))
    fed = fed.astype(F32)
    col, halo = call(
        column_kernel,
        (shape((own * lines, levels, LANES), F32), shape((own * lines + 1, levels, LANES), BF16)),
        [VMEM] * 4,
        (VMEM, VMEM),
    )(cot.reshape(-1, LANES), fed.reshape(-1, LANES), depth, params)
    south = lax.ppermute(halo, "tile", across)
    north = lax.ppermute(halo, "tile", within)
    groups = [
        [(x * CHIPS_Z + z) * CORES + core for z in reversed(range(CHIPS_Z))] for x in range(CHIPS_X) for core in range(CORES)
    ]
    own_parts = lax.all_to_all(line_sum, "tile", 0, 0, axis_index_groups=groups, tiled=True)
    tracer_grad = call(
        mixing_kernel,
        shape((own * levels * lines, LANES), F32),
        [VMEM] * 5,
        HBM,
        [
            pltpu.VMEM((levels // SUB, 5, lines // ROWS, SUB, LANES), F32),
            pltpu.VMEM((levels // SUB, 4, lines // ROWS, SUB, LANES), F32),
            pltpu.VMEM((own * levels * lines, LANES), F32),
            pltpu.SemaphoreType.DMA((own,)),
        ],
        pl.CostEstimate(flops=1_000_000, bytes_accessed=2_000_000, transcendentals=0),
    )(col, south, north, depth, params)
    own_parts, tracer_grad = lax.optimization_barrier((own_parts, tracer_grad))
    tile = lax.axis_index("tile")
    place = (tile // (CHIPS_Z * CORES)) * CORES + tile % CORES
    own_parts = own_parts.reshape(CHIPS_Z, CHIPS_X * CORES, own)
    mine = lax.broadcasted_iota(jnp.int32, own_parts.shape, 1) == place
    rate_grad = jnp.sum(jnp.where(mine, own_parts, 0.0), axis=(0, 1))[None]
    tracer_grad = tracer_grad.reshape(own, levels, lines, LANES)
    return (undense(tracer_grad, band_rows), rate_grad)


def solution(mesh):
    return jax.shard_map(
        body,
        mesh=mesh,
        in_specs=(
            P("trc", None, "tile", None),
            P("trc", None, "tile", None),
            P(None, "tile", None),
            P("tile", None),
            P("tile", None),
            P(),
            P(None, "trc"),
            P("trc"),
            P("trc"),
            P("trc"),
        ),
        out_specs=(P("trc", None, "tile", None), P("tile", "trc")),
        check_vma=False,
    )
```

```python
import jax
import jax.numpy as jnp
from jax import lax
from jax.experimental import pallas as pl
from jax.experimental.pallas import tpu as pltpu
from jax.sharding import PartitionSpec as P

SCALE = 256.0
LANES = 128
ROWS = 2
SUB = 8
CHIPS_X, CHIPS_Z, CORES = 4, 8, 2
BF16 = jnp.bfloat16
F32 = jnp.float32
VMEM = pl.BlockSpec(memory_space=pltpu.VMEM)
HBM = pl.BlockSpec(memory_space=pltpu.HBM)
PARAMS = pltpu.CompilerParams(vmem_limit_bytes=40 * 1024 * 1024)


def row(ref, *at):
    *lead, r = at
    blocks = ref.shape[-2] // ROWS
    return ref[(*lead, pl.ds(r, blocks, stride=ROWS), slice(None))]


def wet_at(depth, level):
    return (depth > level).astype(F32)


def weighted_kernel(
    cot_hbm, nutrient_hbm, depth_hbm, region_hbm, rates_hbm, half_hbm, sinking_hbm, mixing_hbm,
    out_ref, params_ref, nutrient_ref, depth_ref, region_ref,
    cot_ref, rates_ref, half_ref, sinking_ref, mixing_ref, held_ref, sems, out_sems,
):
    own, sunlit = held_ref.shape[1], held_ref.shape[0]
    blocks = cot_ref.shape[2] // ROWS
    pairs = [
        (depth_hbm, depth_ref), (region_hbm, region_ref), (rates_hbm, rates_ref), (nutrient_hbm, nutrient_ref),
        (half_hbm, half_ref), (sinking_hbm, sinking_ref), (mixing_hbm, mixing_ref),
    ]
    cuts = [(0, 3), (3, own)]
    pairs += [(cot_hbm.at[a:b, 0:sunlit], cot_ref.at[a:b]) for a, b in cuts]
    copies = [pltpu.make_async_copy(here, there, sems.at[n]) for n, (here, there) in enumerate(pairs)]
    for copy in copies:
        copy.start()
    for copy in copies[: -len(cuts)]:
        copy.wait()
    depth = [row(depth_ref, r) for r in range(ROWS)]
    region = [row(region_ref, r) for r in range(ROWS)]
    outs = []
    rest = jnp.zeros((1, LANES - rates_ref.shape[1]), F32)
    for t in range(own):
        line = jnp.concatenate([rates_ref[t : t + 1, :], rest], axis=1)
        line = jnp.broadcast_to(line, (blocks, LANES))
        rates = [jnp.take_along_axis(line, region[r], axis=1) for r in range(ROWS)]
        half = half_ref[t]
        for n, ref in enumerate((half_ref, sinking_ref, mixing_ref)):
            params_ref[n * SUB + t : n * SUB + t + 1, :] = jnp.full((1, LANES), ref[t], F32)
        for n, (a, _) in enumerate(cuts):
            if t == a:
                copies[n - len(cuts)].wait()
        for k in range(sunlit):
            rows = []
            for r in range(ROWS):
                food = row(nutrient_ref, k, r)
                limiter = food / (food + half)
                grad = row(cot_ref, t, k, r) * wet_at(depth[r], k)
                rows.append(rates[r] * limiter * grad)
            held_ref[k, t] = jnp.concatenate(rows, axis=0).astype(BF16)
        for n, (a, b) in enumerate(cuts):
            if t == b - 1:
                outs.append(pltpu.make_async_copy(held_ref.at[:, a:b], out_ref.at[:, a:b], out_sems.at[n]))
                outs[-1].start()
    for copy in outs:
        copy.wait()


def province_kernel(cot_ref, uptake_ref, nutrient_ref, depth_ref, region_ref, params_ref, matrix_ref, out_ref, turned_ref, hot_ref, term_ref, parts_ref):
    provinces, own = out_ref.shape

    def reversed_blocks(m):
        return jnp.concatenate([m[i : i + own] for i in range(m.shape[0] - own, -1, -own)], axis=0)

    turned_ref[...] = reversed_blocks(reversed_blocks(matrix_ref[...].astype(F32)).T).astype(BF16)
    sunlit = nutrient_ref.shape[0]
    lines = depth_ref.shape[0]
    depth = depth_ref[...]
    term_ref[...] = jnp.zeros(term_ref.shape, F32)
    for t in range(own):
        half = jnp.broadcast_to(params_ref[t : t + 1, :], (lines, LANES))
        total = jnp.zeros((lines, LANES), F32)
        for k in range(sunlit):
            food = nutrient_ref[k]
            limiter = food / (food + half)
            grad = cot_ref[t, k] * wet_at(depth, k)
            total = total + limiter * uptake_ref[t, k].astype(F32) * grad
        term_ref[pl.ds(t, lines, stride=8), :] = total
    place = lax.broadcasted_iota(jnp.int32, (provinces, LANES), 0)
    z, x, core = CHIPS_Z - 1 - place // (CHIPS_X * CORES), (place // CORES) % CHIPS_X, place % CORES
    ids = (x * CHIPS_Z + z) * CORES + core
    for s in range(lines):
        line = jnp.broadcast_to(region_ref[s : s + 1, :], (provinces, LANES))
        hot_ref[:, s * LANES : (s + 1) * LANES] = (line == ids).astype(F32).astype(BF16)
        term = term_ref[s * 8 : (s + 1) * 8, :]
        high = term.astype(BF16).astype(F32)
        both = jnp.concatenate([high, term - high], axis=0)
        parts_ref[:, s * LANES : (s + 1) * LANES] = both.astype(BF16)
    sums = lax.dot_general(hot_ref[...], parts_ref[...], (((1,), (1,)), ((), ())), preferred_element_type=F32)
    scale = 1.0 / (sunlit * lines * LANES)
    out_ref[...] = (sums[:, 0:own] + sums[:, SUB : SUB + own]) * scale


def feed_kernel(matrix_ref, weighted_ref, out_ref, wide_ref, fed_ref):
    tracers, lines = weighted_ref.shape[0], weighted_ref.shape[1]
    matrix = matrix_ref[...]
    for t in range(tracers):
        wide_ref[t * lines : (t + 1) * lines, :] = weighted_ref[t].astype(F32)
    for s in range(0, lines, 2):
        cells = [wide_ref[pl.ds(s + i, tracers, stride=lines), :].astype(BF16) for i in range(2)]
        fed = jnp.dot(matrix, jnp.concatenate(cells, axis=1), preferred_element_type=F32) * SCALE
        for i in range(2):
            fed_ref[pl.ds(s + i, tracers, stride=lines), :] = fed[:, i * LANES : (i + 1) * LANES]
    for t in range(tracers):
        out_ref[t] = fed_ref[t * lines : (t + 1) * lines, :]


def column_kernel(cot_ref, fed_ref, depth_ref, params_ref, col_ref, halo_ref):
    lines = depth_ref.shape[0]
    blocks = lines // ROWS
    own = col_ref.shape[0] // lines
    levels = col_ref.shape[1]
    blocks_of = [depth_ref[b * ROWS + r : b * ROWS + r + 1, :] for r in range(ROWS) for b in range(blocks)]
    halo_ref[own * lines] = jnp.concatenate(blocks_of, axis=0).astype(F32).astype(BF16)
    ids = lax.broadcasted_iota(jnp.int32, (SUB, LANES), 0)
    bottom = ids == SUB - 1
    for n in range(lines):
        r, b = n // blocks, n % blocks
        depth = jnp.broadcast_to(blocks_of[n], (SUB, LANES))
        top_wet, low_wet = (depth > ids).astype(F32), (depth > ids + SUB).astype(F32)
        top_next = (depth > ids + 1).astype(F32)
        low_next = jnp.where(bottom, 0.0, (depth > ids + SUB + 1).astype(F32))

        for t in range(own):
            base = (t * levels) * lines + b * ROWS + r
            top = cot_ref[pl.ds(base, SUB, stride=lines), :] * top_wet
            low = cot_ref[pl.ds(base + SUB * lines, SUB, stride=lines), :] * low_wet
            fed = fed_ref[pl.ds(t * lines + n, SUB, stride=own * lines), :] * (1.0 / SCALE)
            top = top + top_wet * fed
            low_up = pltpu.roll(low, SUB - 1, 0)
            top_up = jnp.where(bottom, low_up, pltpu.roll(top, SUB - 1, 0))
            sink = params_ref[SUB + t : SUB + t + 1, :]
            col_top = top + sink * top_next * (top_up - top)
            col_low = low + sink * low_next * (low_up - low)
            both = jnp.concatenate([col_top, col_low], axis=0)
            col_ref[t * lines + n] = both
            halo_ref[t * lines + n] = both.astype(BF16)


def mixing_kernel(col_ref, south_ref, north_ref, depth_ref, params_ref, out_hbm, edges_y_ref, edges_x_ref, out_ref, sems):
    lines = depth_ref.shape[0]
    own = col_ref.shape[0] // lines
    blocks = lines // ROWS
    levels = col_ref.shape[1]
    flip = lax.axis_index("tile") & 1
    order = [r ^ flip for r in range(ROWS)]
    halves = levels // SUB
    ids = lax.broadcasted_iota(jnp.int32, (SUB, LANES), 0)
    lane_ids = lax.broadcasted_iota(jnp.int32, (SUB, LANES), 1)
    last_lane, first_lane = lane_ids == LANES - 1, lane_ids == 0

    def east(v):
        turned = [pltpu.roll(x, LANES - 1, 1) for x in v]
        return [jnp.where(last_lane, turned[(b + 1) % blocks], turned[b]) for b in range(blocks)]

    def west(v):
        turned = [pltpu.roll(x, 1, 1) for x in v]
        return [jnp.where(first_lane, turned[(b - 1) % blocks], turned[b]) for b in range(blocks)]

    def own_depth(n):
        r, b = n // blocks, n % blocks
        return jnp.broadcast_to(depth_ref[pl.ds(b * ROWS + order[r], 1), :], (SUB, LANES)).astype(F32)

    def field(which, at, h):
        ref = (south_ref, col_ref, north_ref)[at // ROWS]
        return [ref[which * lines + order[at % ROWS] * blocks + b, h * SUB : (h + 1) * SUB, :].astype(F32) for b in range(blocks)]

    far = [ref[own * lines].astype(F32) for ref in (south_ref, north_ref)]
    far = [jnp.where(flip == 1, jnp.concatenate([x[blocks:], x[:blocks]], axis=0), x) for x in far]
    for h in range(halves):
        at = (ids + h * SUB).astype(F32)
        wet = []
        for i in range(3 * ROWS):
            if i // ROWS == 1:
                depths = [own_depth((i % ROWS) * blocks + b) for b in range(blocks)]
            else:
                band, first = far[i // (2 * ROWS)], (i % ROWS) * blocks
                depths = [jnp.broadcast_to(band[first + b : first + b + 1], (SUB, LANES)) for b in range(blocks)]
            wet.append([(d > at).astype(F32) for d in depths])
        for i in range(3 * ROWS - 1):
            for b in range(blocks):
                edges_y_ref[h, i, b] = wet[i][b] * wet[i + 1][b]
        for i in range(1, 3 * ROWS - 1):
            ahead = east(wet[i])
            for b in range(blocks):
                edges_x_ref[h, i - 1, b] = wet[i][b] * ahead[b]

    def laplacian(rows, h, lo, hi):
        flux = [[edges_y_ref[h, i, b] * (rows[i + 1][b] - rows[i][b]) for b in range(blocks)] for i in range(lo - 1, hi)]
        out = []
        for n, i in enumerate(range(lo, hi)):
            ahead = east(rows[i])
            zonal = [edges_x_ref[h, i - 1, b] * (ahead[b] - rows[i][b]) for b in range(blocks)]
            behind = west(zonal)
            out.append([(flux[n + 1][b] - flux[n][b]) + (zonal[b] - behind[b]) for b in range(blocks)])
        return out

    def copy_out(t):
        part = pl.ds(t * levels * lines, levels * lines)
        return pltpu.make_async_copy(out_ref.at[part], out_hbm.at[part], sems.at[t])

    @pl.loop(0, own)
    def _(t):
        mixing = jnp.broadcast_to(params_ref[pl.ds(2 * SUB + t, 1), :], (SUB, LANES))
        for h in range(halves):
            rows = [field(t, i, h) for i in range(3 * ROWS)]
            once = laplacian(rows, h, 1, 5)
            twice = laplacian([None] + once, h, 2, 4)
            for r in range(ROWS):
                for b in range(blocks):
                    value = rows[ROWS + r][b] - mixing * twice[r][b]
                    out_ref[pl.ds((t * levels + h * SUB) * lines + b * ROWS + order[r], SUB, stride=lines), :] = value
        copy_out(t).start()

    for t in range(own):
        copy_out(t).wait()


def dense(band):
    *lead, rows, zonal = band.shape
    cut = band.reshape(*lead, rows, zonal // LANES, LANES)
    return jnp.swapaxes(cut, -3, -2).reshape(*lead, rows * zonal // LANES, LANES)


def undense(lines, rows):
    *lead, count, _ = lines.shape
    cut = lines.reshape(*lead, count // rows, rows, LANES)
    return jnp.swapaxes(cut, -3, -2).reshape(*lead, rows, count * LANES // rows)


def call(kernel, shapes, ins, outs, scratch=(), cost=None):
    return pl.pallas_call(
        kernel,
        out_shape=shapes,
        in_specs=ins,
        out_specs=outs,
        scratch_shapes=scratch,
        cost_estimate=cost,
        compiler_params=PARAMS,
    )


def body(
    cotangent,
    uptake_rate,
    nutrient,
    depth_levels,
    region_ids,
    uptake_matrix,
    province_rates,
    half_saturation,
    biharmonic,
    sinking,
):
    own, levels, band_rows, zonal = cotangent.shape
    sunlit = uptake_rate.shape[1]
    columns = band_rows * zonal
    lines = columns // LANES
    provinces = province_rates.shape[0]
    tracers = uptake_matrix.shape[0]
    tiles = lax.axis_size("tile")
    within = [(i, i ^ 1) for i in range(tiles)]
    across = [(i, ((i + 1) ^ 1) - 1) for i in range(1, tiles - 1)]
    shape = jax.ShapeDtypeStruct
    cot, uptake, nutrient = dense(cotangent), dense(uptake_rate), dense(nutrient)
    depth, region = dense(depth_levels), dense(region_ids)

    inputs = (cot, nutrient, depth, region, province_rates.T, half_saturation, sinking, biharmonic)
    weighted, params, nutrient, depth, region = call(
        weighted_kernel,
        (
            shape((sunlit, own, lines, LANES), BF16),
            shape((3 * SUB, LANES), F32),
            shape(nutrient.shape, F32),
            shape(depth.shape, jnp.int32),
            shape(region.shape, jnp.int32),
        ),
        [HBM] * 8,
        (HBM,) + (VMEM,) * 4,
        [
            pltpu.VMEM((own, sunlit, lines, LANES), F32),
            pltpu.VMEM((own, provinces), F32),
            pltpu.SMEM((own,), F32),
            pltpu.SMEM((own,), F32),
            pltpu.SMEM((own,), F32),
            pltpu.VMEM((sunlit, own, lines, LANES), BF16),
            pltpu.SemaphoreType.DMA((own + 7,)),
            pltpu.SemaphoreType.DMA((own,)),
        ],
        None,
    )(*(pltpu.with_memory_space_constraint(a, pltpu.HBM) for a in inputs))
    order_y = [list(reversed(range(lax.axis_size("trc"))))]
    all_tracers = lax.all_to_all(weighted, "trc", 0, 0, axis_index_groups=order_y, tiled=True).reshape(tracers, lines, LANES)
    province_part, turned = call(
        province_kernel,
        (shape((provinces, own), F32), shape(uptake_matrix.shape, BF16)),
        [VMEM] * 7,
        (VMEM,) * 2,
        [
            pltpu.VMEM((provinces, columns), BF16),
            pltpu.VMEM((lines * SUB, LANES), F32),
            pltpu.VMEM((2 * SUB, columns), BF16),
        ],
    )(cot, uptake, nutrient, depth, region, params, uptake_matrix)
    def exchanged(part, step):
        return part + lax.ppermute(part, "tile", [(i, i ^ step) for i in range(tiles)])

    chip_sum = exchanged(province_part, 1)
    other_half = lax.ppermute(chip_sum, "tile", [(i, i ^ (CHIPS_Z * CORES)) for i in range(tiles)])
    all_tracers, _ = lax.optimization_barrier((all_tracers, chip_sum))
    fed = call(
        feed_kernel,
        shape((tracers, lines, LANES), F32),
        [VMEM, VMEM],
        VMEM,
        [pltpu.VMEM((tracers * lines, LANES), F32), pltpu.VMEM((tracers * lines, LANES), F32)],
    )(turned, all_tracers)
    fed = fed.astype(jnp.float16).reshape(sunlit, own, lines, LANES)
    fed, chip_sum = lax.optimization_barrier((fed, chip_sum))
    half_sum = chip_sum + other_half
    fed, half_sum = lax.optimization_barrier((fed, half_sum))
    line_sum = exchanged(half_sum, 2 * CHIPS_Z * CORES)
    fed = lax.all_to_all(fed, "trc", 0, 0, axis_index_groups=order_y, tiled=True)
    fed, _ = lax.optimization_barrier((fed, line_sum))
    fed = fed.astype(F32)
    col, halo = call(
        column_kernel,
        (shape((own * lines, levels, LANES), F32), shape((own * lines + 1, levels, LANES), BF16)),
        [VMEM] * 4,
        (VMEM, VMEM),
    )(cot.reshape(-1, LANES), fed.reshape(-1, LANES), depth, params)
    south = lax.ppermute(halo, "tile", across)
    north = lax.ppermute(halo, "tile", within)
    groups = [
        [(x * CHIPS_Z + z) * CORES + core for z in reversed(range(CHIPS_Z))] for x in range(CHIPS_X) for core in range(CORES)
    ]
    own_parts = lax.all_to_all(line_sum, "tile", 0, 0, axis_index_groups=groups, tiled=True)
    tracer_grad = call(
        mixing_kernel,
        shape((own * levels * lines, LANES), F32),
        [VMEM] * 5,
        HBM,
        [
            pltpu.VMEM((levels // SUB, 5, lines // ROWS, SUB, LANES), F32),
            pltpu.VMEM((levels // SUB, 4, lines // ROWS, SUB, LANES), F32),
            pltpu.VMEM((own * levels * lines, LANES), F32),
            pltpu.SemaphoreType.DMA((own,)),
        ],
        pl.CostEstimate(flops=1_000_000, bytes_accessed=2_000_000, transcendentals=0),
    )(col, south, north, depth, params)
    own_parts, tracer_grad = lax.optimization_barrier((own_parts, tracer_grad))
    tile = lax.axis_index("tile")
    place = (tile // (CHIPS_Z * CORES)) * CORES + tile % CORES
    own_parts = own_parts.reshape(CHIPS_Z, CHIPS_X * CORES, own)
    mine = lax.broadcasted_iota(jnp.int32, own_parts.shape, 1) == place
    rate_grad = jnp.sum(jnp.where(mine, own_parts, 0.0), axis=(0, 1))[None]
    tracer_grad = tracer_grad.reshape(own, levels, lines, LANES)
    return (undense(tracer_grad, band_rows), rate_grad)


def solution(mesh):
    return jax.shard_map(
        body,
        mesh=mesh,
        in_specs=(
            P("trc", None, "tile", None),
            P("trc", None, "tile", None),
            P(None, "tile", None),
            P("tile", None),
            P("tile", None),
            P(),
            P(None, "trc"),
            P("trc"),
            P("trc"),
            P("trc"),
        ),
        out_specs=(P("trc", None, "tile", None), P("tile", "trc")),
        check_vma=False,
    )
```

```python
import jax
import jax.numpy as jnp
from jax import lax
from jax.experimental import pallas as pl
from jax.experimental.pallas import tpu as pltpu
from jax.sharding import PartitionSpec as P

SCALE = 256.0
LANES = 128
ROWS = 2
SUB = 8
CHIPS_X, CHIPS_Z, CORES = 4, 8, 2
BF16 = jnp.bfloat16
F32 = jnp.float32
VMEM = pl.BlockSpec(memory_space=pltpu.VMEM)
HBM = pl.BlockSpec(memory_space=pltpu.HBM)
PARAMS = pltpu.CompilerParams(vmem_limit_bytes=40 * 1024 * 1024)


def row(ref, *at):
    *lead, r = at
    blocks = ref.shape[-2] // ROWS
    return ref[(*lead, pl.ds(r, blocks, stride=ROWS), slice(None))]


def wet_at(depth, level):
    return (depth > level).astype(F32)


def weighted_kernel(
    cot_hbm, nutrient_hbm, depth_hbm, region_hbm, rates_hbm, half_hbm, sinking_hbm, mixing_hbm,
    out_ref, params_ref, nutrient_ref, depth_ref, region_ref,
    cot_ref, rates_ref, half_ref, sinking_ref, mixing_ref, held_ref, sems, out_sems,
):
    own, sunlit = held_ref.shape[1], held_ref.shape[0]
    blocks = cot_ref.shape[2] // ROWS
    pairs = [
        (depth_hbm, depth_ref), (region_hbm, region_ref), (rates_hbm, rates_ref), (nutrient_hbm, nutrient_ref),
        (half_hbm, half_ref), (sinking_hbm, sinking_ref), (mixing_hbm, mixing_ref),
    ]
    cuts = [(0, 3), (3, own)]
    pairs += [(cot_hbm.at[a:b, 0:sunlit], cot_ref.at[a:b]) for a, b in cuts]
    copies = [pltpu.make_async_copy(here, there, sems.at[n]) for n, (here, there) in enumerate(pairs)]
    for copy in copies:
        copy.start()
    for copy in copies[: -len(cuts)]:
        copy.wait()
    depth = [row(depth_ref, r) for r in range(ROWS)]
    region = [row(region_ref, r) for r in range(ROWS)]
    outs = []
    rest = jnp.zeros((1, LANES - rates_ref.shape[1]), F32)
    for t in range(own):
        line = jnp.concatenate([rates_ref[t : t + 1, :], rest], axis=1)
        line = jnp.broadcast_to(line, (blocks, LANES))
        rates = [jnp.take_along_axis(line, region[r], axis=1) for r in range(ROWS)]
        half = half_ref[t]
        for n, ref in enumerate((half_ref, sinking_ref, mixing_ref)):
            params_ref[n * SUB + t : n * SUB + t + 1, :] = jnp.full((1, LANES), ref[t], F32)
        for n, (a, _) in enumerate(cuts):
            if t == a:
                copies[n - len(cuts)].wait()
        for k in range(sunlit):
            rows = []
            for r in range(ROWS):
                food = row(nutrient_ref, k, r)
                limiter = food / (food + half)
                grad = row(cot_ref, t, k, r) * wet_at(depth[r], k)
                rows.append(rates[r] * limiter * grad)
            held_ref[k, t] = jnp.concatenate(rows, axis=0).astype(BF16)
        for n, (a, b) in enumerate(cuts):
            if t == b - 1:
                outs.append(pltpu.make_async_copy(held_ref.at[:, a:b], out_ref.at[:, a:b], out_sems.at[n]))
                outs[-1].start()
    for copy in outs:
        copy.wait()


def province_kernel(cot_ref, uptake_ref, nutrient_ref, depth_ref, region_ref, params_ref, matrix_ref, out_ref, turned_ref, hot_ref, term_ref, parts_ref):
    own, provinces = out_ref.shape

    def reversed_blocks(m):
        return jnp.concatenate([m[i : i + own] for i in range(m.shape[0] - own, -1, -own)], axis=0)

    turned_ref[...] = reversed_blocks(reversed_blocks(matrix_ref[...].astype(F32)).T).astype(BF16)
    sunlit = nutrient_ref.shape[0]
    lines = depth_ref.shape[0]
    depth = depth_ref[...]
    term_ref[...] = jnp.zeros(term_ref.shape, F32)
    for t in range(own):
        half = jnp.broadcast_to(params_ref[t : t + 1, :], (lines, LANES))
        total = jnp.zeros((lines, LANES), F32)
        for k in range(sunlit):
            food = nutrient_ref[k]
            limiter = food / (food + half)
            grad = cot_ref[t, k] * wet_at(depth, k)
            total = total + limiter * uptake_ref[t, k].astype(F32) * grad
        term_ref[pl.ds(t, lines, stride=8), :] = total
    place = lax.broadcasted_iota(jnp.int32, (provinces, LANES), 0)
    z, x, core = CHIPS_Z - 1 - place // (CHIPS_X * CORES), (place // CORES) % CHIPS_X, place % CORES
    ids = (x * CHIPS_Z + z) * CORES + core
    for s in range(lines):
        line = jnp.broadcast_to(region_ref[s : s + 1, :], (provinces, LANES))
        hot_ref[:, s * LANES : (s + 1) * LANES] = (line == ids).astype(F32).astype(BF16)
        term = term_ref[s * 8 : (s + 1) * 8, :]
        high = term.astype(BF16).astype(F32)
        both = jnp.concatenate([high, term - high], axis=0)
        parts_ref[:, s * LANES : (s + 1) * LANES] = both.astype(BF16)
    sums = lax.dot_general(parts_ref[...], hot_ref[...], (((1,), (1,)), ((), ())), preferred_element_type=F32)
    scale = 1.0 / (sunlit * lines * LANES)
    out_ref[...] = (sums[0:own] + sums[SUB : SUB + own]) * scale


def feed_kernel(matrix_ref, weighted_ref, out_ref, wide_ref, fed_ref):
    tracers, lines = weighted_ref.shape[0], weighted_ref.shape[1]
    matrix = matrix_ref[...]
    for t in range(tracers):
        wide_ref[t * lines : (t + 1) * lines, :] = weighted_ref[t].astype(F32)
    for s in range(0, lines, 2):
        cells = [wide_ref[pl.ds(s + i, tracers, stride=lines), :].astype(BF16) for i in range(2)]
        fed = jnp.dot(matrix, jnp.concatenate(cells, axis=1), preferred_element_type=F32) * SCALE
        for i in range(2):
            fed_ref[pl.ds(s + i, tracers, stride=lines), :] = fed[:, i * LANES : (i + 1) * LANES]
    for t in range(tracers):
        out_ref[t] = fed_ref[t * lines : (t + 1) * lines, :]


def column_kernel(cot_ref, fed_ref, depth_ref, params_ref, col_ref, halo_ref):
    lines = depth_ref.shape[0]
    blocks = lines // ROWS
    own = col_ref.shape[0] // lines
    levels = col_ref.shape[1]
    blocks_of = [depth_ref[b * ROWS + r : b * ROWS + r + 1, :] for r in range(ROWS) for b in range(blocks)]
    halo_ref[own * lines] = jnp.concatenate(blocks_of, axis=0).astype(F32).astype(BF16)
    ids = lax.broadcasted_iota(jnp.int32, (SUB, LANES), 0)
    bottom = ids == SUB - 1
    for n in range(lines):
        r, b = n // blocks, n % blocks
        depth = jnp.broadcast_to(blocks_of[n], (SUB, LANES))
        top_wet, low_wet = (depth > ids).astype(F32), (depth > ids + SUB).astype(F32)
        top_next = (depth > ids + 1).astype(F32)
        low_next = jnp.where(bottom, 0.0, (depth > ids + SUB + 1).astype(F32))

        for t in range(own):
            base = (t * levels) * lines + b * ROWS + r
            top = cot_ref[pl.ds(base, SUB, stride=lines), :] * top_wet
            low = cot_ref[pl.ds(base + SUB * lines, SUB, stride=lines), :] * low_wet
            fed = fed_ref[pl.ds(t * lines + n, SUB, stride=own * lines), :] * (1.0 / SCALE)
            top = top + top_wet * fed
            low_up = pltpu.roll(low, SUB - 1, 0)
            top_up = jnp.where(bottom, low_up, pltpu.roll(top, SUB - 1, 0))
            sink = params_ref[SUB + t : SUB + t + 1, :]
            col_top = top + sink * top_next * (top_up - top)
            col_low = low + sink * low_next * (low_up - low)
            both = jnp.concatenate([col_top, col_low], axis=0)
            col_ref[t * lines + n] = both
            halo_ref[t * lines + n] = both.astype(BF16)


def mixing_kernel(col_ref, south_ref, north_ref, depth_ref, params_ref, out_hbm, edges_y_ref, edges_x_ref, out_ref, sems):
    lines = depth_ref.shape[0]
    own = col_ref.shape[0] // lines
    blocks = lines // ROWS
    levels = col_ref.shape[1]
    flip = lax.axis_index("tile") & 1
    order = [r ^ flip for r in range(ROWS)]
    halves = levels // SUB
    ids = lax.broadcasted_iota(jnp.int32, (SUB, LANES), 0)
    lane_ids = lax.broadcasted_iota(jnp.int32, (SUB, LANES), 1)
    last_lane, first_lane = lane_ids == LANES - 1, lane_ids == 0

    def east(v):
        turned = [pltpu.roll(x, LANES - 1, 1) for x in v]
        return [jnp.where(last_lane, turned[(b + 1) % blocks], turned[b]) for b in range(blocks)]

    def west(v):
        turned = [pltpu.roll(x, 1, 1) for x in v]
        return [jnp.where(first_lane, turned[(b - 1) % blocks], turned[b]) for b in range(blocks)]

    def own_depth(n):
        r, b = n // blocks, n % blocks
        return jnp.broadcast_to(depth_ref[pl.ds(b * ROWS + order[r], 1), :], (SUB, LANES)).astype(F32)

    def field(which, at, h):
        ref = (south_ref, col_ref, north_ref)[at // ROWS]
        return [ref[which * lines + order[at % ROWS] * blocks + b, h * SUB : (h + 1) * SUB, :].astype(F32) for b in range(blocks)]

    far = [ref[own * lines].astype(F32) for ref in (south_ref, north_ref)]
    far = [jnp.where(flip == 1, jnp.concatenate([x[blocks:], x[:blocks]], axis=0), x) for x in far]
    for h in range(halves):
        at = (ids + h * SUB).astype(F32)
        wet = []
        for i in range(3 * ROWS):
            if i // ROWS == 1:
                depths = [own_depth((i % ROWS) * blocks + b) for b in range(blocks)]
            else:
                band, first = far[i // (2 * ROWS)], (i % ROWS) * blocks
                depths = [jnp.broadcast_to(band[first + b : first + b + 1], (SUB, LANES)) for b in range(blocks)]
            wet.append([(d > at).astype(F32) for d in depths])
        for i in range(3 * ROWS - 1):
            for b in range(blocks):
                edges_y_ref[h, i, b] = wet[i][b] * wet[i + 1][b]
        for i in range(1, 3 * ROWS - 1):
            ahead = east(wet[i])
            for b in range(blocks):
                edges_x_ref[h, i - 1, b] = wet[i][b] * ahead[b]

    def laplacian(rows, h, lo, hi):
        flux = [[edges_y_ref[h, i, b] * (rows[i + 1][b] - rows[i][b]) for b in range(blocks)] for i in range(lo - 1, hi)]
        out = []
        for n, i in enumerate(range(lo, hi)):
            ahead = east(rows[i])
            zonal = [edges_x_ref[h, i - 1, b] * (ahead[b] - rows[i][b]) for b in range(blocks)]
            behind = west(zonal)
            out.append([(flux[n + 1][b] - flux[n][b]) + (zonal[b] - behind[b]) for b in range(blocks)])
        return out

    def copy_out(t):
        part = pl.ds(t * levels * lines, levels * lines)
        return pltpu.make_async_copy(out_ref.at[part], out_hbm.at[part], sems.at[t])

    @pl.loop(0, own)
    def _(t):
        mixing = jnp.broadcast_to(params_ref[pl.ds(2 * SUB + t, 1), :], (SUB, LANES))
        for h in range(halves):
            rows = [field(t, i, h) for i in range(3 * ROWS)]
            once = laplacian(rows, h, 1, 5)
            twice = laplacian([None] + once, h, 2, 4)
            for r in range(ROWS):
                for b in range(blocks):
                    value = rows[ROWS + r][b] - mixing * twice[r][b]
                    out_ref[pl.ds((t * levels + h * SUB) * lines + b * ROWS + order[r], SUB, stride=lines), :] = value
        copy_out(t).start()

    for t in range(own):
        copy_out(t).wait()


def dense(band):
    *lead, rows, zonal = band.shape
    cut = band.reshape(*lead, rows, zonal // LANES, LANES)
    return jnp.swapaxes(cut, -3, -2).reshape(*lead, rows * zonal // LANES, LANES)


def undense(lines, rows):
    *lead, count, _ = lines.shape
    cut = lines.reshape(*lead, count // rows, rows, LANES)
    return jnp.swapaxes(cut, -3, -2).reshape(*lead, rows, count * LANES // rows)


def call(kernel, shapes, ins, outs, scratch=(), cost=None):
    return pl.pallas_call(
        kernel,
        out_shape=shapes,
        in_specs=ins,
        out_specs=outs,
        scratch_shapes=scratch,
        cost_estimate=cost,
        compiler_params=PARAMS,
    )


def body(
    cotangent,
    uptake_rate,
    nutrient,
    depth_levels,
    region_ids,
    uptake_matrix,
    province_rates,
    half_saturation,
    biharmonic,
    sinking,
):
    own, levels, band_rows, zonal = cotangent.shape
    sunlit = uptake_rate.shape[1]
    columns = band_rows * zonal
    lines = columns // LANES
    provinces = province_rates.shape[0]
    tracers = uptake_matrix.shape[0]
    tiles = lax.axis_size("tile")
    within = [(i, i ^ 1) for i in range(tiles)]
    across = [(i, ((i + 1) ^ 1) - 1) for i in range(1, tiles - 1)]
    shape = jax.ShapeDtypeStruct
    cot, uptake, nutrient = dense(cotangent), dense(uptake_rate), dense(nutrient)
    depth, region = dense(depth_levels), dense(region_ids)

    inputs = (cot, nutrient, depth, region, province_rates.T, half_saturation, sinking, biharmonic)
    weighted, params, nutrient, depth, region = call(
        weighted_kernel,
        (
            shape((sunlit, own, lines, LANES), BF16),
            shape((3 * SUB, LANES), F32),
            shape(nutrient.shape, F32),
            shape(depth.shape, jnp.int32),
            shape(region.shape, jnp.int32),
        ),
        [HBM] * 8,
        (HBM,) + (VMEM,) * 4,
        [
            pltpu.VMEM((own, sunlit, lines, LANES), F32),
            pltpu.VMEM((own, provinces), F32),
            pltpu.SMEM((own,), F32),
            pltpu.SMEM((own,), F32),
            pltpu.SMEM((own,), F32),
            pltpu.VMEM((sunlit, own, lines, LANES), BF16),
            pltpu.SemaphoreType.DMA((own + 7,)),
            pltpu.SemaphoreType.DMA((own,)),
        ],
        None,
    )(*(pltpu.with_memory_space_constraint(a, pltpu.HBM) for a in inputs))
    order_y = [list(reversed(range(lax.axis_size("trc"))))]
    all_tracers = lax.all_to_all(weighted, "trc", 0, 0, axis_index_groups=order_y, tiled=True).reshape(tracers, lines, LANES)
    province_part, turned = call(
        province_kernel,
        (shape((own, provinces), F32), shape(uptake_matrix.shape, BF16)),
        [VMEM] * 7,
        (VMEM,) * 2,
        [
            pltpu.VMEM((provinces, columns), BF16),
            pltpu.VMEM((lines * SUB, LANES), F32),
            pltpu.VMEM((2 * SUB, columns), BF16),
        ],
    )(cot, uptake, nutrient, depth, region, params, uptake_matrix)
    def exchanged(part, step):
        return part + lax.ppermute(part, "tile", [(i, i ^ step) for i in range(tiles)])

    chip_sum = exchanged(province_part, 1)
    other_half = lax.ppermute(chip_sum, "tile", [(i, i ^ (CHIPS_Z * CORES)) for i in range(tiles)])
    all_tracers, _ = lax.optimization_barrier((all_tracers, chip_sum))
    fed = call(
        feed_kernel,
        shape((tracers, lines, LANES), F32),
        [VMEM, VMEM],
        VMEM,
        [pltpu.VMEM((tracers * lines, LANES), F32), pltpu.VMEM((tracers * lines, LANES), F32)],
    )(turned, all_tracers)
    fed = fed.astype(jnp.float16).reshape(sunlit, own, lines, LANES)
    fed, chip_sum = lax.optimization_barrier((fed, chip_sum))
    half_sum = chip_sum + other_half
    fed, half_sum = lax.optimization_barrier((fed, half_sum))
    line_sum = exchanged(half_sum, 2 * CHIPS_Z * CORES)
    fed = lax.all_to_all(fed, "trc", 0, 0, axis_index_groups=order_y, tiled=True)
    fed, _ = lax.optimization_barrier((fed, line_sum))
    fed = fed.astype(F32)
    col, halo = call(
        column_kernel,
        (shape((own * lines, levels, LANES), F32), shape((own * lines + 1, levels, LANES), BF16)),
        [VMEM] * 4,
        (VMEM, VMEM),
    )(cot.reshape(-1, LANES), fed.reshape(-1, LANES), depth, params)
    south = lax.ppermute(halo, "tile", across)
    north = lax.ppermute(halo, "tile", within)
    groups = [
        [(x * CHIPS_Z + z) * CORES + core for z in reversed(range(CHIPS_Z))] for x in range(CHIPS_X) for core in range(CORES)
    ]
    own_parts = lax.all_to_all(line_sum.T, "tile", 0, 0, axis_index_groups=groups, tiled=True)
    tracer_grad = call(
        mixing_kernel,
        shape((own * levels * lines, LANES), F32),
        [VMEM] * 5,
        HBM,
        [
            pltpu.VMEM((levels // SUB, 5, lines // ROWS, SUB, LANES), F32),
            pltpu.VMEM((levels // SUB, 4, lines // ROWS, SUB, LANES), F32),
            pltpu.VMEM((own * levels * lines, LANES), F32),
            pltpu.SemaphoreType.DMA((own,)),
        ],
        pl.CostEstimate(flops=1_000_000, bytes_accessed=2_000_000, transcendentals=0),
    )(col, south, north, depth, params)
    own_parts, tracer_grad = lax.optimization_barrier((own_parts, tracer_grad))
    tile = lax.axis_index("tile")
    place = (tile // (CHIPS_Z * CORES)) * CORES + tile % CORES
    own_parts = own_parts.reshape(CHIPS_Z, CHIPS_X * CORES, own)
    mine = lax.broadcasted_iota(jnp.int32, own_parts.shape, 1) == place
    rate_grad = jnp.sum(jnp.where(mine, own_parts, 0.0), axis=(0, 1))[None]
    tracer_grad = tracer_grad.reshape(own, levels, lines, LANES)
    return (undense(tracer_grad, band_rows), rate_grad)


def solution(mesh):
    return jax.shard_map(
        body,
        mesh=mesh,
        in_specs=(
            P("trc", None, "tile", None),
            P("trc", None, "tile", None),
            P(None, "tile", None),
            P("tile", None),
            P("tile", None),
            P(),
            P(None, "trc"),
            P("trc"),
            P("trc"),
            P("trc"),
        ),
        out_specs=(P("trc", None, "tile", None), P("tile", "trc")),
        check_vma=False,
    )
```
